32 devices in a mesh: dp: 4 (over y, x), tm: 8 (over z, core).
Axes of the slice: x: 2, y: 2, z: 4, core: 2. Of those that a mesh axis runs over, the one named last changes fastest.
Arguments:
- pixels: bfloat16 [4, 8, 32, 192], P('dp', 'tm'), may hold values from -1 to 1
- counts: int32 [8, 4, 4], P('tm'), may hold values from 7 to 9, as said below
- clip_lengths: int32 [4, 4], P('dp'), may hold values from 1 to 17, 32 in all within a row
- in_weight: bfloat16 [3, 3, 3, 3, 128], replicated, may hold values from -0.625 to 0.625
- in_bias: float32 [128], replicated, may hold values from -3 to 3
- norm1_gain: float32 [128], replicated, may hold values from 0.5 to 1.5
- norm1_bias: float32 [128], replicated, may hold values from -3 to 3
- conv1_weight: bfloat16 [3, 3, 3, 128, 128], replicated, may hold values from -0.109375 to 0.109375
- norm2_gain: float32 [128], replicated, may hold values from 0.5 to 1.5
- norm2_bias: float32 [128], replicated, may hold values from -3 to 3
- conv2_weight: bfloat16 [3, 3, 3, 128, 128], replicated, may hold values from -0.109375 to 0.109375
- down_weight: bfloat16 [3, 3, 128, 128], replicated, may hold values from -0.1875 to 0.1875
Outputs:
- latents: bfloat16 [4, 8, 32, 2048], P('dp', 'tm')
The draws below stay inside these ranges and needn't reach their ends.
Inputs may be any that keep to these rules, and one draw needn't show every extreme that they name: For each time block, every row and every column of counts sums to 32, and every row holds exactly one entry equal to 9. `clip_lengths`: each row sums to 32, and its longest clip has exactly 17 frames.
All inputs are finite; a program needn't handle non-finite values.
Results may differ from the reference program's by a relative error of at most 0.011.
Values may be sent and summed in bfloat16 or wider, within the bound.
A program may use at most 128 MiB of HBM per device.

```python
import math
import jax
import jax.numpy as jnp
import numpy as np
from jax import lax

CH = 128
GROUPS = 32
FT = 4
HS = 32
PW = 16
RB = 4
KC = 4
U = 32
MOSTF = 17
N_DP = 4
N_TM = 8


def draw_counts(key, part):
    key = jax.random.fold_in(key, 7)
    keys = jax.random.split(key, N_TM)
    places = jnp.arange(N_DP, dtype=jnp.int32)

    def one_block(sub):
        first, second = jax.random.split(sub)
        order = jax.random.permutation(first, N_DP).astype(jnp.int32)
        turn = jax.random.randint(second, (), 1, N_DP).astype(jnp.int32)
        other = jnp.take(order, (places + turn) % N_DP)
        more = (order[:, None] == places[None, :]).astype(jnp.int32)
        fewer = (other[:, None] == places[None, :]).astype(jnp.int32)
        return U // N_DP + more - fewer
    return jax.vmap(one_block)(keys).astype(jnp.int32)


def shard_levels(stream_key, dims, cuts, smallest, top_value):
    level = 1.0
    for axis_at, blocks in cuts:
        draws = jax.random.uniform(jax.random.fold_in(jax.random.fold_in(stream_key, 6), axis_at), (blocks,), jnp.float32, smallest / len(cuts), top_value / len(cuts))
        level = level * jnp.repeat(jnp.exp(draws), dims[axis_at] // blocks).reshape((-1,) + (1,) * (len(dims) - 1 - axis_at))
    return level


def profile(amount, total, most, slope):
    loads = [(1 << 20) // math.isqrt(grade ** slope) + 1 for grade in range(2, amount + 1)]
    surplus, given = total - most - (amount - 1), [1] * (amount - 1)
    while surplus > 0:
        free = [i for i in range(amount - 1) if given[i] < most]
        mass, remaining = sum([loads[i] for i in free]), surplus
        for i in free:
            more = min(most - given[i], max(1, remaining * loads[i] // mass), surplus)
            given[i] = given[i] + more
            surplus = surplus - more
    return np.array([most] + given)


def uneven_parts(stream_key, amount, total, limit, slope):
    if amount == 2:
        one = jax.random.randint(stream_key, (), max(1, total - limit), min(limit, total - 1) + 1)
        return jnp.stack([one, total - one])
    tallies = jnp.asarray(profile(amount, total, limit, slope), jnp.int32)
    twos = (amount - 1) // 2
    donor, receiver = tallies[1:1 + 2 * twos:2], tallies[2:2 + 2 * twos:2]
    slack = jnp.minimum(donor - 1, limit - receiver)
    shifted = jax.random.randint(jax.random.fold_in(stream_key, 1), (twos,), 0, 1 << 20) % (slack + 1)
    tallies = tallies.at[1:1 + 2 * twos:2].set(donor - shifted).at[2:2 + 2 * twos:2].set(receiver + shifted)
    return tallies[jax.random.permutation(jax.random.fold_in(stream_key, 2), amount)]


def bell_draw(stream_key, shape, deviation, limit, held_as=jnp.bfloat16):
    return jnp.clip(deviation * jax.random.normal(stream_key, shape, jnp.float32), -limit, limit).astype(held_as)


def setup_inputs(seed: int = 0) -> dict:
    splits = jax.random.split(jax.random.key(seed), 13)
    return {
        "pixels": jnp.clip(jax.random.uniform(splits[0], (N_DP, N_TM, U, RB * PW * 3), jnp.float32, -1.0, 1.0) * shard_levels(splits[0], (N_DP, N_TM, U, RB * PW * 3), ((0, 4), (1, 8)), -0.4, 0.0), -1.0, 1.0).astype(jnp.bfloat16),
        "counts": draw_counts(jax.random.fold_in(splits[12], 71), 0),
        "clip_lengths": jax.vmap(lambda own: uneven_parts(own, KC, FT * N_TM, MOSTF, 2))(jax.random.split(splits[2], N_DP)).reshape((N_DP, KC)).astype(jnp.int32),
        "in_weight": bell_draw(splits[3], (3, 3, 3, 3, CH), 81 ** -0.5, 0.625),
        "in_bias": bell_draw(splits[4], (CH,), 0.5, 3.0, jnp.float32),
        "norm1_gain": jnp.clip(1.0 + 0.1 * jax.random.normal(splits[5], (CH,), jnp.float32), 0.5, 1.5),
        "norm1_bias": bell_draw(splits[6], (CH,), 0.5, 3.0, jnp.float32),
        "conv1_weight": bell_draw(splits[7], (3, 3, 3, CH, CH), (27 * CH) ** -0.5, 0.109375),
        "norm2_gain": jnp.clip(1.0 + 0.1 * jax.random.normal(splits[8], (CH,), jnp.float32), 0.5, 1.5),
        "norm2_bias": bell_draw(splits[9], (CH,), 0.5, 3.0, jnp.float32),
        "conv2_weight": bell_draw(splits[10], (3, 3, 3, CH, CH), (27 * CH) ** -0.5, 0.109375),
        "down_weight": bell_draw(splits[11], (3, 3, CH, CH), (9 * CH) ** -0.5, 0.1875),
    }


EPS = 1e-06
HIGH = lax.Precision.HIGHEST

def causal_conv(frames, begin, weight):
    count, height, width, chans = frames.shape
    index = jnp.arange(count, dtype=jnp.int32)
    padded = jnp.pad(frames, ((0, 0), (1, 1), (1, 1), (0, 0)))
    total = jnp.zeros((count * height * width, weight.shape[-1]), jnp.float32)
    for lag in range(3):
        picks = jnp.maximum(index - lag, begin).astype(jnp.int32)
        chosen = jnp.take(padded, picks, axis=0)
        for row in range(3):
            band = chosen[:, row:row + height]
            patch = jnp.concatenate([band[:, :, col:col + width] for col in range(3)], axis=-1)
            total = total + jnp.dot(patch.reshape(-1, 3 * chans), weight[2 - lag, row].reshape(3 * chans, -1), preferred_element_type=jnp.float32)
    return total.reshape(count, height, width, -1)

def norm_silu(values, onehot, lengths, gain, bias):
    count, height, width, chans = values.shape
    share = chans // GROUPS
    size = lengths.astype(jnp.float32) * (height * width * share)
    wide = values.astype(jnp.float32)
    sums = lax.optimization_barrier(jnp.sum(wide, axis=(1, 2))).reshape(count, GROUPS, share).sum(-1)
    mean = jnp.dot(onehot.T, sums, precision=HIGH) / size[:, None]
    mean_frame = jnp.repeat(jnp.dot(onehot, mean, precision=HIGH), share, axis=1)
    centered = wide - mean_frame[:, None, None, :]
    dev = lax.optimization_barrier(jnp.sum(centered * centered, axis=(1, 2))).reshape(count, GROUPS, share).sum(-1)
    var = jnp.dot(onehot.T, dev, precision=HIGH) / size[:, None]
    scale = jnp.repeat(jnp.dot(onehot, lax.rsqrt(var + EPS), precision=HIGH), share, axis=1)
    return jax.nn.silu(centered * scale[:, None, None, :] * gain + bias).astype(jnp.bfloat16)

def shrink(values, weight):
    count, height, width, chans = values.shape
    padded = jnp.pad(values, ((0, 0), (0, 1), (0, 1), (0, 0)))
    total = jnp.zeros((count * (height // 2) * (width // 2), weight.shape[-1]), jnp.float32)
    for row in range(3):
        band = padded[:, row:row + height:2]
        patch = jnp.concatenate([band[:, :, col:col + width:2] for col in range(3)], axis=-1)
        total = total + jnp.dot(patch.reshape(-1, 3 * chans), weight[row].reshape(3 * chans, -1), preferred_element_type=jnp.float32)
    return total.reshape(count, height // 2, width // 2, -1)

def reference(pixels, counts, clip_lengths, in_weight, in_bias, norm1_gain, norm1_bias, conv1_weight, norm2_gain, norm2_bias, conv2_weight, down_weight):
    places = jnp.arange(U, dtype=jnp.int32)
    enc_ids = jnp.arange(N_DP, dtype=jnp.int32)
    columns = []
    for block in range(N_TM):
        table = counts[block].astype(jnp.int32)
        send_start = (jnp.cumsum(table, axis=1) - table).astype(jnp.int32)
        recv_end = jnp.cumsum(table, axis=0).astype(jnp.int32)
        recv_start = (recv_end - table).astype(jnp.int32)
        source = lax.optimization_barrier(jnp.sum((recv_end.T[:, None, :] <= places[None, :, None]).astype(jnp.int32), axis=2)).astype(jnp.int32)
        spot = send_start[source, enc_ids[:, None]] + places[None, :] - recv_start[source, enc_ids[:, None]]
        columns.append(pixels[source, block, spot])
    routed = jnp.stack(columns, axis=1)
    frames_all = routed.reshape(N_DP, N_TM * FT, HS, PW, 3)

    def encode(item):
        frames, lengths = item
        lengths = lengths.astype(jnp.int32)
        ends = jnp.cumsum(lengths).astype(jnp.int32)
        starts = (ends - lengths).astype(jnp.int32)
        index = jnp.arange(frames.shape[0], dtype=jnp.int32)
        ident = lax.optimization_barrier(jnp.sum((ends[None, :] <= index[:, None]).astype(jnp.int32), axis=1)).astype(jnp.int32)
        begin = jnp.take(starts, ident).astype(jnp.int32)
        onehot = (ident[:, None] == jnp.arange(lengths.shape[0], dtype=jnp.int32)[None, :]).astype(jnp.float32)
        base = (causal_conv(frames, begin, in_weight) + in_bias).astype(jnp.bfloat16)
        act1 = norm_silu(base, onehot, lengths, norm1_gain, norm1_bias)
        middle = causal_conv(act1, begin, conv1_weight).astype(jnp.bfloat16)
        act2 = norm_silu(middle, onehot, lengths, norm2_gain, norm2_bias)
        resid = (base.astype(jnp.float32) + causal_conv(act2, begin, conv2_weight)).astype(jnp.bfloat16)
        return shrink(resid, down_weight).astype(jnp.bfloat16)
    encoded = lax.map(encode, (frames_all, clip_lengths))
    enc_units = encoded.reshape(N_DP, N_TM, U, -1)
    outputs = []
    for block in range(N_TM):
        table = counts[block].astype(jnp.int32)
        send_end = jnp.cumsum(table, axis=1).astype(jnp.int32)
        send_start = (send_end - table).astype(jnp.int32)
        recv_start = (jnp.cumsum(table, axis=0) - table).astype(jnp.int32)
        owner = lax.optimization_barrier(jnp.sum((send_end[:, None, :] <= places[None, :, None]).astype(jnp.int32), axis=2)).astype(jnp.int32)
        loaders = enc_ids[:, None]
        spot = recv_start[loaders, owner] + places[None, :] - send_start[loaders, owner]
        outputs.append(enc_units[owner, block, spot])
    return jnp.stack(outputs, axis=1)
```

```python
import functools

import jax
import jax.numpy as jnp
import numpy as np
from jax import lax
from jax.experimental import pallas as pl
from jax.experimental.pallas import tpu as pltpu
from jax.sharding import PartitionSpec as P

GROUPS = 32
HS = 32
PW = 16
RB = 4
CH = 128
LAGS = 3
EPS = 1e-06
MESH = pl.DeviceIdType.MESH
BF = jnp.bfloat16
F32 = jnp.float32
WIDE = 256
ROW = PW * 3
PIX = HS * PW


def tap_columns():
    table = np.full((LAGS * WIDE, CH), -100, np.int32)
    for kt in range(LAGS):
        for dy in range(3):
            for col in range(PW):
                for color in range(3):
                    r = kt * WIDE + dy * ROW + col * 3 + color
                    for dx in range(3):
                        table[r, ((kt * 3 + dy) * 3 + dx) * 3 + color] = col + 1 - dx
    return table


def group_sum(x):
    lane = lax.broadcasted_iota(jnp.int32, x.shape, 1)
    for step in (1, 2):
        ahead = pltpu.roll(x, CH - step, axis=1)
        behind = pltpu.roll(x, step, axis=1)
        x = x + jnp.where((lane & step) == 0, ahead, behind)
    return x


def kernel(
    n_dp,
    n_tm,
    counts,
    lengths,
    pixels,
    columns,
    in_w,
    vecs,
    w1_hbm,
    w2_hbm,
    wd_hbm,
    out,
    w1,
    w2,
    wd,
    toeplitz,
    placed,
    pix_in,
    pix_rows,
    xrows,
    lhs,
    base,
    mid,
    act,
    resid,
    mid_send,
    mid_halo,
    stats1,
    stats2,
    latent,
    packed,
    returned,
    gathered,
    w_sem,
    px_send,
    px_recv,
    st_send,
    st_recv,
    halo_send,
    halo_recv,
    back_send,
    back_recv,
):
    units = pixels.shape[0]
    per_frame = HS // RB
    span = units // per_frame
    cap = units // n_dp + 1
    me = lax.axis_index("dp")
    t = lax.axis_index("tm")
    clips = lengths.shape[0]

    barrier = pltpu.get_barrier_semaphore()

    def greet(d, column):
        pl.semaphore_signal(barrier, inc=1, device_id=(d, column), device_id_type=MESH)

    for k in range(1, n_tm):
        greet(me, lax.rem(t + k, n_tm))
    for k in range(1, n_dp):
        d = lax.rem(me + k, n_dp)
        greet(d, t)

        @pl.when(t > 0)
        def _():
            greet(d, t - 1)

        @pl.when(t < n_tm - 1)
        def _():
            greet(d, t + 1)

    weight_copies = [
        pltpu.make_async_copy(src, dst, w_sem.at[i])
        for i, (src, dst) in enumerate(((w1_hbm, w1), (w2_hbm, w2), (wd_hbm, wd)))
    ]
    for copy in weight_copies:
        copy.start()

    def recv_start_of(d, e):
        total = jnp.int32(0)
        for other in range(n_dp):
            total = total + jnp.where(other < d, counts[other, e], 0)
        return total

    send_start, send_end = [], []
    running = jnp.int32(0)
    for e in range(n_dp):
        send_start.append(running)
        running = running + counts[me, e]
        send_end.append(running)

    place_r = lax.broadcasted_iota(jnp.int32, (units, units), 0)
    place_i = lax.broadcasted_iota(jnp.int32, (units, units), 1)
    mine = pixels[...]
    for e in range(n_dp):
        turn = recv_start_of(me, e) - send_start[e]
        hit = (place_r == place_i + turn) & (place_i >= send_start[e]) & (place_i < send_end[e])
        placed[e] = jnp.dot(
            hit.astype(F32).astype(BF), mine, preferred_element_type=F32
        ).astype(BF)

    at_edge = (t == 0) | (t == n_tm - 1)

    @pl.when(at_edge)
    def _():
        pl.semaphore_wait(barrier, n_tm - 1 + 2 * (n_dp - 1))

    @pl.when(jnp.logical_not(at_edge))
    def _():
        pl.semaphore_wait(barrier, n_tm - 1 + 3 * (n_dp - 1))

    def pixel_copy(e, ahead):
        return pltpu.make_async_remote_copy(
            src_ref=placed.at[e],
            dst_ref=pix_in.at[1 - ahead, me],
            send_sem=px_send.at[ahead, e],
            recv_sem=px_recv.at[1 - ahead, me],
            device_id=(e, t + ahead),
            device_id_type=MESH,
        )

    for k in range(n_dp):
        e = lax.rem(me + k, n_dp)

        @pl.when(t < n_tm - 1)
        def _():
            pixel_copy(e, 1).start()

        if k:
            pixel_copy(e, 0).start()
    pix_in[1, me] = placed[me]

    @pl.when(t == 0)
    def _():
        pix_in[0] = jnp.zeros(pix_in.shape[1:], BF)
        mid_halo[...] = jnp.zeros(mid_halo.shape, BF)

    place = columns[...]
    weight_in = in_w[...]
    for col in range(PW):
        pick = jnp.where(place == col, 1.0, 0.0).astype(BF)
        toeplitz[:, col * CH : (col + 1) * CH] = jnp.dot(
            pick, weight_in, preferred_element_type=F32
        ).astype(BF)
    for j in range(span + 2):
        act[j, 0] = jnp.zeros((PW, 3 * CH), BF)
        act[j, HS + 1] = jnp.zeros((PW, 3 * CH), BF)
    resid[span * PIX : span * PIX + 16, :] = jnp.zeros((16, CH), F32)

    start = t * span
    ends, begins = [], []
    running = jnp.int32(0)
    for k in range(clips):
        begins.append(running)
        running = running + lengths[k]
        ends.append(running)

    def clip_of(g):
        first, last = begins[0], ends[0]
        for k in range(1, clips):
            later = ends[k - 1] <= g
            first = jnp.where(later, begins[k], first)
            last = jnp.where(later, ends[k], last)
        return first, last

    frame_clip = [clip_of(start - 2 + j) for j in range(span + 2)]

    def picked(j, lag, lead):
        g = start - 2 + j
        return jnp.maximum(g - lag, frame_clip[j][0]) - (start - lead)

    for k in range(1, n_dp):
        d = lax.rem(me + k, n_dp)
        pltpu.make_async_copy(pix_in.at[1, d], pix_in.at[1, d], px_recv.at[1, d]).wait()

    @pl.when(t > 0)
    def _():
        for d in range(n_dp):
            pltpu.make_async_copy(pix_in.at[0, d], pix_in.at[0, d], px_recv.at[0, d]).wait()

    whole = []
    for half in range(2):
        total = pix_in[half, 0].astype(F32)
        for d in range(1, n_dp):
            total = total + pix_in[half, d].astype(F32)
        whole.append(total)
    whole = jnp.concatenate(whole, axis=0)
    lane = lax.broadcasted_iota(jnp.int32, whole.shape, 1)
    for q in range(RB):
        shifted = pltpu.roll(whole, (ROW - q * ROW) % WIDE, axis=1)
        rows = jnp.where((lane >= ROW) & (lane < 2 * ROW), shifted, 0.0)
        for half in range(2):
            pix_rows[half, pl.ds(q, 2 * units, stride=RB), :] = rows[:, half * CH : (half + 1) * CH]
    rows = jnp.concatenate([pix_rows[0], pix_rows[1]], axis=1)
    place = lax.broadcasted_iota(jnp.int32, rows.shape, 0) & (HS - 1)
    count = rows.shape[0]
    above = jnp.where(place == 0, 0.0, pltpu.roll(rows, 1, axis=0))
    below = jnp.where(place == HS - 1, 0.0, pltpu.roll(rows, count - 1, axis=0))
    rows = rows + pltpu.roll(above, WIDE - ROW, axis=1) + pltpu.roll(below, ROW, axis=1)
    xrows[...] = rows.astype(BF).reshape(2 * span, HS, WIDE)

    for j in range(span + 2):
        for kt in range(LAGS):
            lhs[j * HS : (j + 1) * HS, kt * WIDE : (kt + 1) * WIDE] = xrows[picked(j, 2 - kt, 4)]
    patch = lhs[...]
    for col in range(PW):
        part = jnp.dot(
            patch, toeplitz[:, col * CH : (col + 1) * CH], preferred_element_type=F32
        )
        part = (part + vecs[0:1, :]).astype(BF).astype(F32)
        base[pl.ds(col, (span + 2) * HS, stride=PW), :] = part

    def frame_stats(x):
        total = jnp.sum(x, axis=0, keepdims=True)
        away = x - total * (1.0 / PIX)
        return total, jnp.sum(away * away, axis=0, keepdims=True)

    def share_stats(stats, which, rows):
        stats[t] = jnp.concatenate([r[0] for r in rows] + [r[1] for r in rows], axis=0)
        copies = []
        for k in range(1, n_tm):
            other = lax.rem(t + k, n_tm)
            copy = pltpu.make_async_remote_copy(
                src_ref=stats.at[t],
                dst_ref=stats.at[t],
                send_sem=st_send.at[which, k],
                recv_sem=st_recv.at[which, t],
                device_id=(me, other),
                device_id_type=MESH,
            )
            copy.start()
            copies.append(copy)
        return copies

    def norm_terms(stats, which, copies):
        for k in range(1, n_tm):
            other = lax.rem(t + k, n_tm)
            pltpu.make_async_copy(stats.at[other], stats.at[other], st_recv.at[which, other]).wait()
        sums = jnp.concatenate([stats[i, 0:span] for i in range(n_tm)], axis=0)
        devs = jnp.concatenate([stats[i, span : 2 * span] for i in range(n_tm)], axis=0)
        g = lax.broadcasted_iota(jnp.int32, sums.shape, 0)
        share = CH // GROUPS
        inside, sizes, means = [], [], []
        for first, last in frame_clip:
            hit = (g >= first) & (g < last)
            inside.append(hit)
            sizes.append((last - first).astype(F32) * (PIX * share))
            means.append(jnp.sum(jnp.where(hit, sums, 0.0), axis=0, keepdims=True))
        pad = [jnp.zeros((8 - len(means), CH), F32)] if len(means) < 8 else []
        means = group_sum(jnp.concatenate(means + pad, axis=0))
        means = [means[j : j + 1] / sizes[j] for j in range(span + 2)]
        frame_mean = sums * (1.0 / PIX)
        spread = []
        for j in range(span + 2):
            off = frame_mean - means[j]
            spread.append(
                jnp.sum(jnp.where(inside[j], devs + PIX * off * off, 0.0), axis=0, keepdims=True)
            )
        spread = group_sum(jnp.concatenate(spread + pad, axis=0))
        scales = [lax.rsqrt(spread[j : j + 1] / sizes[j] + EPS) for j in range(span + 2)]
        return means, scales

    column = lax.broadcasted_iota(jnp.int32, (PIX, CH), 0) & (PW - 1)

    def activate(j, x, mean, scale, gain, bias):
        y = (x - mean) * (scale * gain) + bias
        y = 0.5 * y
        y = y + y * jnp.tanh(y)
        left = jnp.where(column == 0, 0.0, pltpu.roll(y, 1, axis=0))
        right = jnp.where(column == PW - 1, 0.0, pltpu.roll(y, PIX - 1, axis=0))
        for i, part in enumerate((left, y, right)):
            act[j, 1 : HS + 1, :, i * CH : (i + 1) * CH] = part.astype(BF).reshape(HS, PW, CH)

    def conv_frame(j, weight):
        taps = []
        for kt in range(LAGS):
            p = picked(j, 2 - kt, 2)
            for dy in range(3):
                taps.append(act[p, dy : dy + HS].reshape(PIX, 3 * CH))
        return jnp.dot(jnp.concatenate(taps, axis=1), weight[...], preferred_element_type=F32)

    rows = [frame_stats(base[(j + 2) * PIX : (j + 3) * PIX, :]) for j in range(span)]
    stat_copies = share_stats(stats1, 0, rows)
    means, scales = norm_terms(stats1, 0, stat_copies)
    for j in range(span + 2):
        activate(
            j, base[j * PIX : (j + 1) * PIX, :], means[j], scales[j], vecs[1:2, :], vecs[2:3, :]
        )
    weight_copies[0].wait()

    halo = pltpu.make_async_remote_copy(
        src_ref=mid_send,
        dst_ref=mid_halo,
        send_sem=halo_send,
        recv_sem=halo_recv,
        device_id=(me, t + 1),
        device_id_type=MESH,
    )
    rows = [None] * span
    order = list(range(span - 2, span)) + list(range(span - 2))
    for at, j in enumerate(order):
        x = conv_frame(j + 2, w1).astype(BF)
        if at < 2:
            mid_send[at] = x
        x = x.astype(F32)
        mid[j * PIX : (j + 1) * PIX, :] = x
        rows[j] = frame_stats(x)
        if at == 1:

            @pl.when(t < n_tm - 1)
            def _():
                halo.start()

    stat_copies2 = share_stats(stats2, 1, rows)
    means, scales = norm_terms(stats2, 1, stat_copies2)
    for j in range(span):
        activate(
            j + 2,
            mid[j * PIX : (j + 1) * PIX, :],
            means[j + 2],
            scales[j + 2],
            vecs[3:4, :],
            vecs[4:5, :],
        )

    @pl.when(t > 0)
    def _():
        halo.wait_recv()

    for j in range(2):
        activate(
            j, mid_halo[j].astype(F32), means[j], scales[j], vecs[3:4, :], vecs[4:5, :]
        )
    weight_copies[1].wait()
    for j in range(span):
        x = conv_frame(j + 2, w2) + base[(j + 2) * PIX : (j + 3) * PIX, :]
        resid[j * PIX : (j + 1) * PIX, :] = x.astype(BF).astype(F32)

    weight_copies[2].wait()
    half = PW // 2
    cells = span * HS * half
    spot = lax.broadcasted_iota(jnp.int32, (cells, CH), 0) & (half - 1)
    taps = [None] * 9
    for kx in range(3):
        x = resid[pl.ds(kx, cells, stride=2), :]
        if kx == 2:
            x = jnp.where(spot == half - 1, 0.0, x)
        x = x.reshape(span, HS // 2, 2, half, CH)
        even, odd = x[:, :, 0], x[:, :, 1]
        after = jnp.concatenate(
            [even[:, 1:], jnp.zeros((span, 1, half, CH), F32)], axis=1
        )
        for ky, rows in enumerate((even, odd, after)):
            taps[ky * 3 + kx] = rows.reshape(cells // 2, CH).astype(BF)
    encoded = jnp.dot(jnp.concatenate(taps, axis=1), wd[...], preferred_element_type=F32).astype(BF)
    unit_rows = RB * PW // 4
    latent[0:units] = encoded.reshape(units, unit_rows, CH)
    latent[units:] = jnp.zeros((cap, unit_rows, CH), BF)

    back = []
    for k in range(n_dp):
        d = lax.rem(me + k, n_dp)
        block = latent[pl.ds(recv_start_of(d, me), cap)]
        if k == 0:
            returned[me] = block
        else:
            packed[k] = block
            copy = pltpu.make_async_remote_copy(
                src_ref=packed.at[k],
                dst_ref=returned.at[me],
                send_sem=back_send.at[k],
                recv_sem=back_recv.at[me],
                device_id=(d, t),
                device_id_type=MESH,
            )
            copy.start()
            back.append(copy)
    for k in range(1, n_dp):
        d = lax.rem(me + k, n_dp)
        pltpu.make_async_copy(returned.at[d], returned.at[d], back_recv.at[d]).wait()
    for p in range(units):
        owner = jnp.int32(0)
        first = jnp.int32(0)
        for e in range(1, n_dp):
            later = send_start[e] <= p
            owner = jnp.where(later, e, owner)
            first = jnp.where(later, send_start[e], first)
        gathered[p * unit_rows : (p + 1) * unit_rows, :] = returned[
            owner, jnp.minimum(p - first, cap - 1)
        ].astype(F32)
    for k in range(unit_rows):
        out[:, k * CH : (k + 1) * CH] = gathered[pl.ds(k, units, stride=unit_rows), :].astype(BF)

    for copy in stat_copies + stat_copies2 + back:
        copy.wait_send()
    for k in range(n_dp):
        e = lax.rem(me + k, n_dp)
        if k:
            pixel_copy(e, 0).wait_send()

    @pl.when(t < n_tm - 1)
    def _():
        halo.wait_send()
        for k in range(n_dp):
            pixel_copy(lax.rem(me + k, n_dp), 1).wait_send()


def per_device(
    pixels,
    counts,
    clip_lengths,
    in_weight,
    in_bias,
    norm1_gain,
    norm1_bias,
    conv1_weight,
    norm2_gain,
    norm2_bias,
    conv2_weight,
    down_weight,
):
    n_dp = lax.axis_size("dp")
    n_tm = lax.axis_size("tm")
    units = pixels.shape[2]
    span = units // (HS // RB)
    cap = units // n_dp + 1
    unit_rows = RB * PW // 4
    mine = jnp.pad(pixels[0, 0], ((0, 0), (0, WIDE - pixels.shape[3])))
    in_w = jnp.pad(in_weight.reshape(27 * 3, CH), ((0, CH - 27 * 3), (0, 0)))
    vecs = jnp.stack([in_bias, norm1_gain, norm1_bias, norm2_gain, norm2_bias])
    vmem = pl.BlockSpec(memory_space=pltpu.VMEM)
    smem = pl.BlockSpec(memory_space=pltpu.SMEM)
    hbm = pl.BlockSpec(memory_space=pl.ANY)
    result = pl.pallas_call(
        functools.partial(kernel, n_dp, n_tm),
        out_shape=jax.ShapeDtypeStruct((units, unit_rows * CH), BF),
        in_specs=[smem, smem, vmem, vmem, vmem, vmem, hbm, hbm, hbm],
        out_specs=vmem,
        scratch_shapes=[
            pltpu.VMEM((27 * CH, CH), BF),
            pltpu.VMEM((27 * CH, CH), BF),
            pltpu.VMEM((9 * CH, CH), BF),
            pltpu.VMEM((LAGS * WIDE, PW * CH), BF),
            pltpu.VMEM((n_dp, units, WIDE), BF),
            pltpu.VMEM((2, n_dp, units, WIDE), BF),
            pltpu.VMEM((2, 2 * units * RB, CH), F32),
            pltpu.VMEM((2 * span, HS, WIDE), BF),
            pltpu.VMEM(((span + 2) * HS, LAGS * WIDE), BF),
            pltpu.VMEM(((span + 2) * PIX, CH), F32),
            pltpu.VMEM((span * PIX, CH), F32),
            pltpu.VMEM((span + 2, HS + 2, PW, 3 * CH), BF),
            pltpu.VMEM((span * PIX + 16, CH), F32),
            pltpu.VMEM((2, PIX, CH), BF),
            pltpu.VMEM((2, PIX, CH), BF),
            pltpu.VMEM((n_tm, 2 * span, CH), F32),
            pltpu.VMEM((n_tm, 2 * span, CH), F32),
            pltpu.VMEM((units + cap, unit_rows, CH), BF),
            pltpu.VMEM((n_dp, cap, unit_rows, CH), BF),
            pltpu.VMEM((n_dp, cap, unit_rows, CH), BF),
            pltpu.VMEM((units * unit_rows, CH), F32),
            pltpu.SemaphoreType.DMA((3,)),
            pltpu.SemaphoreType.DMA((2, n_dp)),
            pltpu.SemaphoreType.DMA((2, n_dp)),
            pltpu.SemaphoreType.DMA((2, n_tm)),
            pltpu.SemaphoreType.DMA((2, n_tm)),
            pltpu.SemaphoreType.DMA(()),
            pltpu.SemaphoreType.DMA(()),
            pltpu.SemaphoreType.DMA((n_dp,)),
            pltpu.SemaphoreType.DMA((n_dp,)),
        ],
        compiler_params=pltpu.CompilerParams(
            collective_id=0, has_side_effects=True, vmem_limit_bytes=48 * 1024 * 1024
        ),
        name="encoder_block",
    )(
        counts[0],
        clip_lengths[0],
        mine,
        jnp.asarray(tap_columns()),
        in_w,
        vecs,
        conv1_weight.reshape(27 * CH, CH),
        conv2_weight.reshape(27 * CH, CH),
        down_weight.reshape(9 * CH, CH),
    )
    return result.reshape(1, 1, units, unit_rows * CH)


def solution(mesh):
    in_specs = (
        P("dp", "tm", None, None),
        P("tm", None, None),
        P("dp", None),
        P(),
        P(),
        P(),
        P(),
        P(),
        P(),
        P(),
        P(),
        P(),
    )
    out_specs = P("dp", "tm", None, None)
    return jax.shard_map(
        per_device, mesh=mesh, in_specs=in_specs, out_specs=out_specs, check_vma=False
    )
```

```python
import functools

import jax
import jax.numpy as jnp
import numpy as np
from jax import lax
from jax.experimental import pallas as pl
from jax.experimental.pallas import tpu as pltpu
from jax.sharding import PartitionSpec as P

GROUPS = 32
HS = 32
PW = 16
RB = 4
CH = 128
LAGS = 3
EPS = 1e-06
MESH = pl.DeviceIdType.MESH
BF = jnp.bfloat16
F32 = jnp.float32
WIDE = 256
ROW = PW * 3
PIX = HS * PW
HALF = PIX // 2
PAIRS = PW // 2
PART = 64


def tap_columns():
    table = np.full((LAGS * WIDE, CH), -100, np.int32)
    for kt in range(LAGS):
        for dy in range(3):
            for col in range(PW):
                for color in range(3):
                    r = kt * WIDE + dy * ROW + col * 3 + color
                    for dx in range(3):
                        table[r, ((kt * 3 + dy) * 3 + dx) * 4 + color] = col + 1 - dx
    return table


def group_sum(x):
    lane = lax.broadcasted_iota(jnp.int32, x.shape, 1)
    for step in (1, 2):
        ahead = pltpu.roll(x, CH - step, axis=1)
        behind = pltpu.roll(x, step, axis=1)
        x = x + jnp.where((lane & step) == 0, ahead, behind)
    return x


def kernel(
    n_dp,
    n_tm,
    counts_hbm,
    lengths_hbm,
    pixels_hbm,
    columns_hbm,
    in_w_hbm,
    bias0_hbm,
    gain1_hbm,
    bias1_hbm,
    gain2_hbm,
    bias2_hbm,
    w1_hbm,
    w2_hbm,
    wd_hbm,
    out,
    counts,
    lengths,
    pixels,
    columns,
    in_w,
    vecs,
    taps_w,
    w1,
    w2,
    wd,
    toeplitz,
    placed,
    pix_in,
    pix_rows,
    xrows,
    lhs,
    base,
    mid,
    act_a,
    act_b,
    resid,
    mid_send,
    mid_halo,
    stats1,
    stats2,
    latent,
    packed,
    returned,
    gathered,
    small_sem,
    w_sem,
    px_send,
    px_recv,
    st_send,
    st_recv,
    halo_send,
    halo_recv,
    back_send,
    back_recv,
):
    units = pixels.shape[0]
    per_frame = HS // RB
    span = units // per_frame
    cap = units // n_dp + 1
    me = lax.axis_index("dp")
    t = lax.axis_index("tm")
    clips = lengths.shape[1]

    barrier = pltpu.get_barrier_semaphore()

    def greet(d, column):
        pl.semaphore_signal(barrier, inc=1, device_id=(d, column), device_id_type=MESH)

    for k in range(1, n_tm):
        greet(me, lax.rem(t + k, n_tm))
    for k in range(1, n_dp):
        d = lax.rem(me + k, n_dp)
        greet(d, t)

        @pl.when(t > 0)
        def _():
            greet(d, t - 1)

        @pl.when(t < n_tm - 1)
        def _():
            greet(d, t + 1)

    small = (
        (pixels_hbm.at[0, 0], pixels),
        (counts_hbm.at[0], counts),
        (columns_hbm, columns),
        (in_w_hbm, in_w),
        (lengths_hbm, lengths),
        (bias0_hbm, vecs.at[0]),
        (gain1_hbm, vecs.at[1]),
        (bias1_hbm, vecs.at[2]),
        (gain2_hbm, vecs.at[3]),
        (bias2_hbm, vecs.at[4]),
    )
    small_copies = [
        pltpu.make_async_copy(src, dst, small_sem.at[i]) for i, (src, dst) in enumerate(small)
    ]
    for copy in small_copies:
        copy.start()
    side = 3 * CH
    large = (
        (w1_hbm, w1.at[:, 0:side, 0:CH]),
        (w1_hbm, w1.at[:, CH : CH + side, CH : 2 * CH]),
        (w2_hbm, w2.at[:, 0:side, 0:CH]),
        (w2_hbm, w2.at[:, CH : CH + side, CH : 2 * CH]),
        (wd_hbm, wd),
    )
    weight_copies = [
        pltpu.make_async_copy(src, dst, w_sem.at[i]) for i, (src, dst) in enumerate(large)
    ]
    for copy in weight_copies:
        copy.start()
    small_copies[0].wait()
    small_copies[1].wait()

    def recv_start_of(d, e):
        total = jnp.int32(0)
        for other in range(n_dp):
            total = total + jnp.where(other < d, counts[other, e], 0)
        return total

    send_start, send_end = [], []
    running = jnp.int32(0)
    for e in range(n_dp):
        send_start.append(running)
        running = running + counts[me, e]
        send_end.append(running)

    place_r = lax.broadcasted_iota(jnp.int32, (units, units), 0)
    place_i = lax.broadcasted_iota(jnp.int32, (units, units), 1)
    mine = pixels[...]
    for e in range(n_dp):
        turn = recv_start_of(me, e) - send_start[e]
        hit = (place_r == place_i + turn) & (place_i >= send_start[e]) & (place_i < send_end[e])
        placed[e, :, 0 : RB * ROW] = jnp.dot(
            hit.astype(F32).astype(BF), mine, preferred_element_type=F32
        ).astype(BF)

    at_edge = (t == 0) | (t == n_tm - 1)

    @pl.when(at_edge)
    def _():
        pl.semaphore_wait(barrier, n_tm - 1 + 2 * (n_dp - 1))

    @pl.when(jnp.logical_not(at_edge))
    def _():
        pl.semaphore_wait(barrier, n_tm - 1 + 3 * (n_dp - 1))

    def pixel_copy(e, ahead):
        return pltpu.make_async_remote_copy(
            src_ref=placed.at[e],
            dst_ref=pix_in.at[1 - ahead, me],
            send_sem=px_send.at[ahead, e],
            recv_sem=px_recv.at[1 - ahead, me],
            device_id=(e, t + ahead),
            device_id_type=MESH,
        )

    for k in range(n_dp):
        e = lax.rem(me + k, n_dp)

        @pl.when(t < n_tm - 1)
        def _():
            pixel_copy(e, 1).start()

        if k:
            pixel_copy(e, 0).start()
    pix_in[1, me] = placed[me]

    @pl.when(t == 0)
    def _():
        pix_in[0] = jnp.zeros(pix_in.shape[1:], BF)
        mid_halo[...] = jnp.zeros(mid_halo.shape, BF)

    for copy in small_copies[2:]:
        copy.wait()
    taps_w[...] = jnp.zeros(taps_w.shape, F32)
    for tap in range(27):
        kt, dy, dx = tap // 9, tap // 3 % 3, tap % 3
        taps_w[4 * tap : 4 * tap + 3, :] = in_w[kt, dy, dx].astype(F32)
    place = columns[...]
    weight_in = taps_w[...].astype(BF)
    for col in range(PW):
        pick = jnp.where(place == col, 1.0, 0.0).astype(BF)
        toeplitz[:, col * CH : (col + 1) * CH] = jnp.dot(
            pick, weight_in, preferred_element_type=F32
        ).astype(BF)
    for weight in (w1, w2):
        weight[:, side : side + CH, 0:CH] = jnp.zeros((9, CH, CH), BF)
        weight[:, 0:CH, CH : 2 * CH] = jnp.zeros((9, CH, CH), BF)

    start = t * span
    ends, begins = [], []
    running = jnp.int32(0)
    for k in range(clips):
        begins.append(running)
        running = running + lengths[0, k]
        ends.append(running)

    def clip_of(g):
        first, last = begins[0], ends[0]
        for k in range(1, clips):
            later = ends[k - 1] <= g
            first = jnp.where(later, begins[k], first)
            last = jnp.where(later, ends[k], last)
        return first, last

    frame_clip = [clip_of(start - 2 + j) for j in range(span + 2)]

    def picked(j, lag, lead):
        g = start - 2 + j
        return jnp.maximum(g - lag, frame_clip[j][0]) - (start - lead)

    for k in range(1, n_dp):
        d = lax.rem(me + k, n_dp)
        pltpu.make_async_copy(pix_in.at[1, d], pix_in.at[1, d], px_recv.at[1, d]).wait()

    @pl.when(t > 0)
    def _():
        for d in range(n_dp):
            pltpu.make_async_copy(pix_in.at[0, d], pix_in.at[0, d], px_recv.at[0, d]).wait()

    whole = []
    for half in range(2):
        total = pix_in[half, 0].astype(F32)
        for d in range(1, n_dp):
            total = total + pix_in[half, d].astype(F32)
        whole.append(total)
    whole = jnp.concatenate(whole, axis=0)
    lane = lax.broadcasted_iota(jnp.int32, whole.shape, 1)
    for q in range(RB):
        shifted = pltpu.roll(whole, (ROW - q * ROW) % WIDE, axis=1)
        rows = jnp.where((lane >= ROW) & (lane < 2 * ROW), shifted, 0.0)
        for half in range(2):
            pix_rows[half, pl.ds(q, 2 * units, stride=RB), :] = rows[:, half * CH : (half + 1) * CH]
    rows = jnp.concatenate([pix_rows[0], pix_rows[1]], axis=1)
    place = lax.broadcasted_iota(jnp.int32, rows.shape, 0) & (HS - 1)
    count = rows.shape[0]
    above = jnp.where(place == 0, 0.0, pltpu.roll(rows, 1, axis=0))
    below = jnp.where(place == HS - 1, 0.0, pltpu.roll(rows, count - 1, axis=0))
    rows = rows + pltpu.roll(above, WIDE - ROW, axis=1) + pltpu.roll(below, ROW, axis=1)
    xrows[...] = rows.astype(BF).reshape(2 * span, HS, WIDE)

    for j in range(span + 2):
        for kt in range(LAGS):
            lhs[j * HS : (j + 1) * HS, kt * WIDE : (kt + 1) * WIDE] = xrows[picked(j, 2 - kt, 4)]
    patch = lhs[...]
    for pair in range(PAIRS):
        both = jnp.dot(
            patch, toeplitz[:, pair * 2 * CH : (pair + 1) * 2 * CH], preferred_element_type=F32
        )
        for side_at in range(2):
            part = both[:, side_at * CH : (side_at + 1) * CH] + vecs[0]
            base[side_at, pl.ds(pair, (span + 2) * HS, stride=PAIRS), :] = part.astype(BF).astype(F32)

    def frame_stats(even, odd):
        total = jnp.sum(even, axis=0, keepdims=True) + jnp.sum(odd, axis=0, keepdims=True)
        mean = total * (1.0 / PIX)
        even, odd = even - mean, odd - mean
        away = jnp.sum(even * even, axis=0, keepdims=True) + jnp.sum(odd * odd, axis=0, keepdims=True)
        return total, away

    def share_stats(stats, which, rows):
        stats[t] = jnp.concatenate([r[0] for r in rows] + [r[1] for r in rows], axis=0)
        copies = []
        for k in range(1, n_tm):
            other = lax.rem(t + k, n_tm)
            copy = pltpu.make_async_remote_copy(
                src_ref=stats.at[t],
                dst_ref=stats.at[t],
                send_sem=st_send.at[which, k],
                recv_sem=st_recv.at[which, t],
                device_id=(me, other),
                device_id_type=MESH,
            )
            copy.start()
            copies.append(copy)
        return copies

    def norm_terms(stats, which, copies):
        for k in range(1, n_tm):
            other = lax.rem(t + k, n_tm)
            pltpu.make_async_copy(stats.at[other], stats.at[other], st_recv.at[which, other]).wait()
        sums = jnp.concatenate([stats[i, 0:span] for i in range(n_tm)], axis=0)
        devs = jnp.concatenate([stats[i, span : 2 * span] for i in range(n_tm)], axis=0)
        g = lax.broadcasted_iota(jnp.int32, sums.shape, 0)
        share = CH // GROUPS
        inside, sizes, means = [], [], []
        for first, last in frame_clip:
            hit = (g >= first) & (g < last)
            inside.append(hit)
            sizes.append((last - first).astype(F32) * (PIX * share))
            means.append(jnp.sum(jnp.where(hit, sums, 0.0), axis=0, keepdims=True))
        pad = [jnp.zeros((8 - len(means), CH), F32)] if len(means) < 8 else []
        means = group_sum(jnp.concatenate(means + pad, axis=0))
        means = [means[j : j + 1] / sizes[j] for j in range(span + 2)]
        frame_mean = sums * (1.0 / PIX)
        spread = []
        for j in range(span + 2):
            off = frame_mean - means[j]
            spread.append(
                jnp.sum(jnp.where(inside[j], devs + PIX * off * off, 0.0), axis=0, keepdims=True)
            )
        spread = group_sum(jnp.concatenate(spread + pad, axis=0))
        scales = [lax.rsqrt(spread[j : j + 1] / sizes[j] + EPS) for j in range(span + 2)]
        return means, scales

    pair_at = lax.broadcasted_iota(jnp.int32, (PART, CH), 0) & (PAIRS - 1)
    blank = jnp.zeros((PAIRS, CH), F32)

    def activate(j, source, first, mean, scale, gain, bias):
        factor = scale * gain
        carry = [blank] * 4
        for at in range(0, HALF, PART):
            done = []
            for side_at in range(2):
                x = source(side_at, first + at)
                y = 0.5 * ((x - mean) * factor + bias)
                done.append(y + y * jnp.tanh(y))
            even, odd = done
            before = jnp.where(pair_at == 0, 0.0, pltpu.roll(odd, 1, axis=0))
            after = jnp.where(pair_at == PAIRS - 1, 0.0, pltpu.roll(even, PART - 1, axis=0))
            for i, part in enumerate((before, even, odd, after)):
                lanes = slice(i * CH, (i + 1) * CH)
                act_b[j, at : at + PART, lanes] = part.astype(BF)
                late = jnp.concatenate([carry[i], part[: PART - PAIRS]], axis=0)
                act_a[j, at : at + PART, lanes] = late.astype(BF)
                carry[i] = part[PART - PAIRS :]
        for i in range(4):
            act_a[j, HALF : HALF + 2 * PAIRS, i * CH : (i + 1) * CH] = jnp.concatenate(
                [carry[i], blank], axis=0
            ).astype(BF)

    def conv_frame(j, weight):
        taps = []
        for kt in range(LAGS):
            p = picked(j, 2 - kt, 2)
            taps += [act_a[p, 0:HALF], act_b[p], act_a[p, 2 * PAIRS : 2 * PAIRS + HALF]]
        both = jnp.dot(
            jnp.concatenate(taps, axis=1),
            weight[...].reshape(9 * 4 * CH, 2 * CH),
            preferred_element_type=F32,
        )
        return both[:, :CH], both[:, CH:]

    rows = [
        frame_stats(*[base[i, (j + 2) * HALF : (j + 3) * HALF, :] for i in range(2)])
        for j in range(span)
    ]
    stat_copies = share_stats(stats1, 0, rows)
    means, scales = norm_terms(stats1, 0, stat_copies)
    for j in range(span + 2):
        activate(
            j, lambda i, at: base[i, at : at + PART, :], j * HALF, means[j], scales[j], vecs[1], vecs[2]
        )
    weight_copies[0].wait()
    weight_copies[1].wait()

    halo = pltpu.make_async_remote_copy(
        src_ref=mid_send,
        dst_ref=mid_halo,
        send_sem=halo_send,
        recv_sem=halo_recv,
        device_id=(me, t + 1),
        device_id_type=MESH,
    )
    rows = [None] * span
    order = list(range(span - 2, span)) + list(range(span - 2))
    for at, j in enumerate(order):
        pieces = []
        for i, x in enumerate(conv_frame(j + 2, w1)):
            x = x.astype(BF)
            if at < 2:
                mid_send[at, i] = x
            x = x.astype(F32)
            mid[i, j * HALF : (j + 1) * HALF, :] = x
            pieces.append(x)
        rows[j] = frame_stats(*pieces)
        if at == 1:

            @pl.when(t < n_tm - 1)
            def _():
                halo.start()

    stat_copies2 = share_stats(stats2, 1, rows)
    means, scales = norm_terms(stats2, 1, stat_copies2)
    for j in range(span):
        activate(
            j + 2,
            lambda i, at: mid[i, at : at + PART, :],
            j * HALF,
            means[j + 2],
            scales[j + 2],
            vecs[3],
            vecs[4],
        )

    @pl.when(t > 0)
    def _():
        halo.wait_recv()

    for j in range(2):
        activate(
            j,
            lambda i, at: mid_halo[j, i, at : at + PART, :].astype(F32),
            0,
            means[j],
            scales[j],
            vecs[3],
            vecs[4],
        )
    weight_copies[2].wait()
    weight_copies[3].wait()
    for j in range(span):
        for i, x in enumerate(conv_frame(j + 2, w2)):
            x = x + base[i, (j + 2) * HALF : (j + 3) * HALF, :]
            resid[i, j * HALF : (j + 1) * HALF, :] = x.astype(BF).astype(F32)

    weight_copies[4].wait()
    cells = span * HALF
    spot = lax.broadcasted_iota(jnp.int32, (cells, CH), 0) & (PAIRS - 1)
    taps = [None] * 9
    even, odd = resid[0], resid[1]
    next_even = jnp.where(spot == PAIRS - 1, 0.0, pltpu.roll(even, cells - 1, axis=0))
    for kx, x in enumerate((even, odd, next_even)):
        x = x.reshape(span, HS // 2, 2, PAIRS, CH)
        upper, lower = x[:, :, 0], x[:, :, 1]
        below = jnp.concatenate([upper[:, 1:], jnp.zeros((span, 1, PAIRS, CH), F32)], axis=1)
        for ky, rows in enumerate((upper, lower, below)):
            taps[ky * 3 + kx] = rows.reshape(cells // 2, CH).astype(BF)
    encoded = jnp.dot(jnp.concatenate(taps, axis=1), wd[...], preferred_element_type=F32).astype(BF)
    unit_rows = RB * PW // 4
    latent[0:units] = encoded.reshape(units, unit_rows, CH)
    latent[units:] = jnp.zeros((cap, unit_rows, CH), BF)

    back = []
    for k in range(n_dp):
        d = lax.rem(me + k, n_dp)
        block = latent[pl.ds(recv_start_of(d, me), cap)]
        if k == 0:
            returned[me] = block
        else:
            packed[k] = block
            copy = pltpu.make_async_remote_copy(
                src_ref=packed.at[k],
                dst_ref=returned.at[me],
                send_sem=back_send.at[k],
                recv_sem=back_recv.at[me],
                device_id=(d, t),
                device_id_type=MESH,
            )
            copy.start()
            back.append(copy)
    for k in range(1, n_dp):
        d = lax.rem(me + k, n_dp)
        pltpu.make_async_copy(returned.at[d], returned.at[d], back_recv.at[d]).wait()
    for p in range(units):
        owner = jnp.int32(0)
        first = jnp.int32(0)
        for e in range(1, n_dp):
            later = send_start[e] <= p
            owner = jnp.where(later, e, owner)
            first = jnp.where(later, send_start[e], first)
        gathered[p * unit_rows : (p + 1) * unit_rows, :] = returned[
            owner, jnp.minimum(p - first, cap - 1)
        ].astype(F32)
    for k in range(unit_rows):
        out[:, k * CH : (k + 1) * CH] = gathered[pl.ds(k, units, stride=unit_rows), :].astype(BF)

    for copy in stat_copies + stat_copies2 + back:
        copy.wait_send()
    for k in range(n_dp):
        e = lax.rem(me + k, n_dp)
        if k:
            pixel_copy(e, 0).wait_send()

    @pl.when(t < n_tm - 1)
    def _():
        halo.wait_send()
        for k in range(n_dp):
            pixel_copy(lax.rem(me + k, n_dp), 1).wait_send()


def per_device(
    pixels,
    counts,
    clip_lengths,
    in_weight,
    in_bias,
    norm1_gain,
    norm1_bias,
    conv1_weight,
    norm2_gain,
    norm2_bias,
    conv2_weight,
    down_weight,
):
    n_dp = lax.axis_size("dp")
    n_tm = lax.axis_size("tm")
    units = pixels.shape[2]
    span = units // (HS // RB)
    cap = units // n_dp + 1
    unit_rows = RB * PW // 4
    vmem = pl.BlockSpec(memory_space=pltpu.VMEM)
    hbm = pl.BlockSpec(memory_space=pltpu.MemorySpace.HBM)
    result = pl.pallas_call(
        functools.partial(kernel, n_dp, n_tm),
        out_shape=jax.ShapeDtypeStruct((units, unit_rows * CH), BF),
        in_specs=[hbm] * 13,
        out_specs=vmem,
        scratch_shapes=[
            pltpu.SMEM((n_dp, n_dp), jnp.int32),
            pltpu.SMEM(clip_lengths.shape, jnp.int32),
            pltpu.VMEM(pixels.shape[2:], BF),
            pltpu.VMEM((LAGS * WIDE, CH), jnp.int32),
            pltpu.VMEM(in_weight.shape, BF),
            pltpu.VMEM((5, 1, CH), F32),
            pltpu.VMEM((CH, CH), F32),
            pltpu.VMEM((9, 4 * CH, 2 * CH), BF),
            pltpu.VMEM((9, 4 * CH, 2 * CH), BF),
            pltpu.VMEM((9 * CH, CH), BF),
            pltpu.VMEM((LAGS * WIDE, PW * CH), BF),
            pltpu.VMEM((n_dp, units, WIDE), BF),
            pltpu.VMEM((2, n_dp, units, WIDE), BF),
            pltpu.VMEM((2, 2 * units * RB, CH), F32),
            pltpu.VMEM((2 * span, HS, WIDE), BF),
            pltpu.VMEM(((span + 2) * HS, LAGS * WIDE), BF),
            pltpu.VMEM((2, (span + 2) * HALF, CH), F32),
            pltpu.VMEM((2, span * HALF, CH), F32),
            pltpu.VMEM((span + 2, HALF + 2 * PAIRS, 4 * CH), BF),
            pltpu.VMEM((span + 2, HALF, 4 * CH), BF),
            pltpu.VMEM((2, span * HALF, CH), F32),
            pltpu.VMEM((2, 2, HALF, CH), BF),
            pltpu.VMEM((2, 2, HALF, CH), BF),
            pltpu.VMEM((n_tm, 2 * span, CH), F32),
            pltpu.VMEM((n_tm, 2 * span, CH), F32),
            pltpu.VMEM((units + cap, unit_rows, CH), BF),
            pltpu.VMEM((n_dp, cap, unit_rows, CH), BF),
            pltpu.VMEM((n_dp, cap, unit_rows, CH), BF),
            pltpu.VMEM((units * unit_rows, CH), F32),
            pltpu.SemaphoreType.DMA((10,)),
            pltpu.SemaphoreType.DMA((5,)),
            pltpu.SemaphoreType.DMA((2, n_dp)),
            pltpu.SemaphoreType.DMA((2, n_dp)),
            pltpu.SemaphoreType.DMA((2, n_tm)),
            pltpu.SemaphoreType.DMA((2, n_tm)),
            pltpu.SemaphoreType.DMA(()),
            pltpu.SemaphoreType.DMA(()),
            pltpu.SemaphoreType.DMA((n_dp,)),
            pltpu.SemaphoreType.DMA((n_dp,)),
        ],
        compiler_params=pltpu.CompilerParams(
            collective_id=0, has_side_effects=True, vmem_limit_bytes=48 * 1024 * 1024
        ),
        name="encoder_block",
    )(
        counts,
        clip_lengths,
        pixels,
        jnp.asarray(tap_columns()),
        in_weight,
        *[v.reshape(1, CH) for v in (in_bias, norm1_gain, norm1_bias, norm2_gain, norm2_bias)],
        conv1_weight.reshape(9, 3 * CH, CH),
        conv2_weight.reshape(9, 3 * CH, CH),
        down_weight.reshape(9 * CH, CH),
    )
    return result.reshape(1, 1, units, unit_rows * CH)


def solution(mesh):
    in_specs = (
        P("dp", "tm", None, None),
        P("tm", None, None),
        P("dp", None),
        P(),
        P(),
        P(),
        P(),
        P(),
        P(),
        P(),
        P(),
        P(),
    )
    out_specs = P("dp", "tm", None, None)
    return jax.shard_map(
        per_device, mesh=mesh, in_specs=in_specs, out_specs=out_specs, check_vma=False
    )
```

```python
import functools

import jax
import jax.numpy as jnp
import numpy as np
from jax import lax
from jax.experimental import pallas as pl
from jax.experimental.pallas import tpu as pltpu
from jax.sharding import PartitionSpec as P

GROUPS = 32
HS = 32
PW = 16
RB = 4
CH = 128
LAGS = 3
EPS = 1e-06
MESH = pl.DeviceIdType.MESH
BF = jnp.bfloat16
F32 = jnp.float32
WIDE = 256
ROW = PW * 3
PIX = HS * PW
HALF = PIX // 2
PAIRS = PW // 2
PART = 64


def tap_columns():
    table = np.full((LAGS * WIDE, CH), -100, np.int32)
    for kt in range(LAGS):
        for dy in range(3):
            for col in range(PW):
                for color in range(3):
                    r = kt * WIDE + dy * ROW + col * 3 + color
                    for dx in range(3):
                        table[r, ((kt * 3 + dy) * 3 + dx) * 4 + color] = col + 1 - dx
    return table


def group_sum(x):
    lane = lax.broadcasted_iota(jnp.int32, x.shape, 1)
    for step in (1, 2):
        ahead = pltpu.roll(x, CH - step, axis=1)
        behind = pltpu.roll(x, step, axis=1)
        x = x + jnp.where((lane & step) == 0, ahead, behind)
    return x


def kernel(
    n_dp,
    n_tm,
    counts_hbm,
    lengths_hbm,
    pixels_hbm,
    columns_hbm,
    in_w_hbm,
    bias0_hbm,
    gain1_hbm,
    bias1_hbm,
    gain2_hbm,
    bias2_hbm,
    w1_hbm,
    w2_hbm,
    wd_hbm,
    out,
    counts,
    lengths,
    pixels,
    columns,
    in_w,
    vecs,
    taps_w,
    w1,
    w2,
    wd,
    toeplitz,
    placed,
    pix_in,
    pix_rows,
    xrows,
    lhs,
    base,
    mid,
    act_a,
    act_b,
    resid,
    mid_send,
    mid_halo,
    stats1,
    stats2,
    latent,
    packed,
    returned,
    gathered,
    small_sem,
    w_sem,
    px_send,
    px_recv,
    st_send,
    st_recv,
    halo_send,
    halo_recv,
    back_send,
    back_recv,
):
    units = pixels.shape[0]
    per_frame = HS // RB
    span = units // per_frame
    cap = units // n_dp + 1
    me = lax.axis_index("dp")
    t = lax.axis_index("tm")
    clips = lengths.shape[1]

    barrier = pltpu.get_barrier_semaphore()

    def greet(d, column):
        pl.semaphore_signal(barrier, inc=1, device_id=(d, column), device_id_type=MESH)

    for k in range(1, n_tm):
        greet(me, lax.rem(t + k, n_tm))
    for k in range(1, n_dp):
        d = lax.rem(me + k, n_dp)
        greet(d, t)

        @pl.when(t > 0)
        def _():
            greet(d, t - 1)

        @pl.when(t < n_tm - 1)
        def _():
            greet(d, t + 1)

    small = (
        (pixels_hbm.at[0, 0], pixels),
        (counts_hbm.at[0], counts),
        (columns_hbm, columns),
        (in_w_hbm, in_w),
        (lengths_hbm, lengths),
        (bias0_hbm, vecs.at[0]),
        (gain1_hbm, vecs.at[1]),
        (bias1_hbm, vecs.at[2]),
        (gain2_hbm, vecs.at[3]),
        (bias2_hbm, vecs.at[4]),
    )
    small_copies = [
        pltpu.make_async_copy(src, dst, small_sem.at[i]) for i, (src, dst) in enumerate(small)
    ]
    for copy in small_copies:
        copy.start()
    side = 3 * CH
    large = (
        (w1_hbm, w1.at[:, 0:side, 0:CH]),
        (w1_hbm, w1.at[:, CH : CH + side, CH : 2 * CH]),
        (w2_hbm, w2.at[:, 0:side, 0:CH]),
        (w2_hbm, w2.at[:, CH : CH + side, CH : 2 * CH]),
        (wd_hbm, wd),
    )
    weight_copies = [
        pltpu.make_async_copy(src, dst, w_sem.at[i]) for i, (src, dst) in enumerate(large)
    ]
    for copy in weight_copies:
        copy.start()
    small_copies[0].wait()
    small_copies[1].wait()

    def recv_start_of(d, e):
        total = jnp.int32(0)
        for other in range(n_dp):
            total = total + jnp.where(other < d, counts[other, e], 0)
        return total

    send_start, send_end = [], []
    running = jnp.int32(0)
    for e in range(n_dp):
        send_start.append(running)
        running = running + counts[me, e]
        send_end.append(running)

    place_r = lax.broadcasted_iota(jnp.int32, (units, units), 0)
    place_i = lax.broadcasted_iota(jnp.int32, (units, units), 1)
    mine = pixels[...]
    for e in range(n_dp):
        turn = recv_start_of(me, e) - send_start[e]
        hit = (place_r == place_i + turn) & (place_i >= send_start[e]) & (place_i < send_end[e])
        placed[e, :, 0 : RB * ROW] = jnp.dot(
            hit.astype(F32).astype(BF), mine, preferred_element_type=F32
        ).astype(BF)

    at_edge = (t == 0) | (t == n_tm - 1)

    @pl.when(at_edge)
    def _():
        pl.semaphore_wait(barrier, n_tm - 1 + 2 * (n_dp - 1))

    @pl.when(jnp.logical_not(at_edge))
    def _():
        pl.semaphore_wait(barrier, n_tm - 1 + 3 * (n_dp - 1))

    def pixel_copy(e, ahead):
        return pltpu.make_async_remote_copy(
            src_ref=placed.at[e],
            dst_ref=pix_in.at[1 - ahead, me],
            send_sem=px_send.at[ahead, e],
            recv_sem=px_recv.at[1 - ahead, me],
            device_id=(e, t + ahead),
            device_id_type=MESH,
        )

    for k in range(n_dp):
        e = lax.rem(me + k, n_dp)

        @pl.when(t < n_tm - 1)
        def _():
            pixel_copy(e, 1).start()

        if k:
            pixel_copy(e, 0).start()
    pix_in[1, me] = placed[me]

    @pl.when(t == 0)
    def _():
        pix_in[0] = jnp.zeros(pix_in.shape[1:], BF)
        mid_halo[...] = jnp.zeros(mid_halo.shape, BF)

    for copy in small_copies[2:]:
        copy.wait()
    taps_w[...] = jnp.zeros(taps_w.shape, F32)
    for tap in range(27):
        kt, dy, dx = tap // 9, tap // 3 % 3, tap % 3
        taps_w[4 * tap : 4 * tap + 3, :] = in_w[kt, dy, dx].astype(F32)
    place = columns[...]
    weight_in = taps_w[...].astype(BF)
    for col in range(PW):
        pick = jnp.where(place == col, 1.0, 0.0).astype(BF)
        toeplitz[:, col * CH : (col + 1) * CH] = jnp.dot(
            pick, weight_in, preferred_element_type=F32
        ).astype(BF)
    for weight in (w1, w2):
        weight[:, side : side + CH, 0:CH] = jnp.zeros((9, CH, CH), BF)
        weight[:, 0:CH, CH : 2 * CH] = jnp.zeros((9, CH, CH), BF)

    start = t * span
    ends, begins = [], []
    running = jnp.int32(0)
    for k in range(clips):
        begins.append(running)
        running = running + lengths[0, k]
        ends.append(running)

    def clip_of(g):
        first, last = begins[0], ends[0]
        for k in range(1, clips):
            later = ends[k - 1] <= g
            first = jnp.where(later, begins[k], first)
            last = jnp.where(later, ends[k], last)
        return first, last

    frame_clip = [clip_of(start - 2 + j) for j in range(span + 2)]

    def picked(j, lag, lead):
        g = start - 2 + j
        return jnp.maximum(g - lag, frame_clip[j][0]) - (start - lead)

    for k in range(1, n_dp):
        d = lax.rem(me + k, n_dp)
        pltpu.make_async_copy(pix_in.at[1, d], pix_in.at[1, d], px_recv.at[1, d]).wait()

    @pl.when(t > 0)
    def _():
        for d in range(n_dp):
            pltpu.make_async_copy(pix_in.at[0, d], pix_in.at[0, d], px_recv.at[0, d]).wait()

    whole = []
    for half in range(2):
        total = pix_in[half, 0].astype(F32)
        for d in range(1, n_dp):
            total = total + pix_in[half, d].astype(F32)
        whole.append(total)
    whole = jnp.concatenate(whole, axis=0)
    lane = lax.broadcasted_iota(jnp.int32, whole.shape, 1)
    for q in range(RB):
        shifted = pltpu.roll(whole, (ROW - q * ROW) % WIDE, axis=1)
        rows = jnp.where((lane >= ROW) & (lane < 2 * ROW), shifted, 0.0)
        for half in range(2):
            pix_rows[half, pl.ds(q, 2 * units, stride=RB), :] = rows[:, half * CH : (half + 1) * CH]
    rows = jnp.concatenate([pix_rows[0], pix_rows[1]], axis=1)
    place = lax.broadcasted_iota(jnp.int32, rows.shape, 0) & (HS - 1)
    count = rows.shape[0]
    above = jnp.where(place == 0, 0.0, pltpu.roll(rows, 1, axis=0))
    below = jnp.where(place == HS - 1, 0.0, pltpu.roll(rows, count - 1, axis=0))
    rows = rows + pltpu.roll(above, WIDE - ROW, axis=1) + pltpu.roll(below, ROW, axis=1)
    xrows[...] = rows.astype(BF).reshape(2 * span, HS, WIDE)

    for j in range(span + 2):
        for kt in range(LAGS):
            lhs[j * HS : (j + 1) * HS, kt * WIDE : (kt + 1) * WIDE] = xrows[picked(j, 2 - kt, 4)]

    def base_frames(first, amount):
        patch = lhs[first * HS : (first + amount) * HS, :]
        for pair in range(PAIRS):
            both = jnp.dot(
                patch, toeplitz[:, pair * 2 * CH : (pair + 1) * 2 * CH], preferred_element_type=F32
            )
            for side_at in range(2):
                part = both[:, side_at * CH : (side_at + 1) * CH] + vecs[0]
                base[side_at, pl.ds(first * HALF + pair, amount * HS, stride=PAIRS), :] = part.astype(
                    BF
                ).astype(F32)

    base_frames(2, span)

    def frame_stats(even, odd):
        total = jnp.sum(even, axis=0, keepdims=True) + jnp.sum(odd, axis=0, keepdims=True)
        mean = total * (1.0 / PIX)
        even, odd = even - mean, odd - mean
        away = jnp.sum(even * even, axis=0, keepdims=True) + jnp.sum(odd * odd, axis=0, keepdims=True)
        return total, away

    def share_stats(stats, which, rows):
        stats[t] = jnp.concatenate([r[0] for r in rows] + [r[1] for r in rows], axis=0)
        copies = []
        for k in range(1, n_tm):
            other = lax.rem(t + k, n_tm)
            copy = pltpu.make_async_remote_copy(
                src_ref=stats.at[t],
                dst_ref=stats.at[t],
                send_sem=st_send.at[which, k],
                recv_sem=st_recv.at[which, t],
                device_id=(me, other),
                device_id_type=MESH,
            )
            copy.start()
            copies.append(copy)
        return copies

    def norm_terms(stats, which, copies):
        for k in range(1, n_tm):
            other = lax.rem(t + k, n_tm)
            pltpu.make_async_copy(stats.at[other], stats.at[other], st_recv.at[which, other]).wait()
        sums = jnp.concatenate([stats[i, 0:span] for i in range(n_tm)], axis=0)
        devs = jnp.concatenate([stats[i, span : 2 * span] for i in range(n_tm)], axis=0)
        g = lax.broadcasted_iota(jnp.int32, sums.shape, 0)
        share = CH // GROUPS
        inside, sizes, means = [], [], []
        for first, last in frame_clip:
            hit = (g >= first) & (g < last)
            inside.append(hit)
            sizes.append((last - first).astype(F32) * (PIX * share))
            means.append(jnp.sum(jnp.where(hit, sums, 0.0), axis=0, keepdims=True))
        pad = [jnp.zeros((8 - len(means), CH), F32)] if len(means) < 8 else []
        means = group_sum(jnp.concatenate(means + pad, axis=0))
        means = [means[j : j + 1] / sizes[j] for j in range(span + 2)]
        frame_mean = sums * (1.0 / PIX)
        spread = []
        for j in range(span + 2):
            off = frame_mean - means[j]
            spread.append(
                jnp.sum(jnp.where(inside[j], devs + PIX * off * off, 0.0), axis=0, keepdims=True)
            )
        spread = group_sum(jnp.concatenate(spread + pad, axis=0))
        scales = [lax.rsqrt(spread[j : j + 1] / sizes[j] + EPS) for j in range(span + 2)]
        return means, scales

    pair_at = lax.broadcasted_iota(jnp.int32, (PART, CH), 0) & (PAIRS - 1)
    blank = jnp.zeros((PAIRS, CH), F32)

    def activate(j, source, first, mean, scale, gain, bias):
        factor = scale * gain
        carry = [blank] * 4
        for at in range(0, HALF, PART):
            done = []
            for side_at in range(2):
                x = source(side_at, first + at)
                y = 0.5 * ((x - mean) * factor + bias)
                done.append(y + y * jnp.tanh(y))
            even, odd = done
            before = jnp.where(pair_at == 0, 0.0, pltpu.roll(odd, 1, axis=0))
            after = jnp.where(pair_at == PAIRS - 1, 0.0, pltpu.roll(even, PART - 1, axis=0))
            for i, part in enumerate((before, even, odd, after)):
                lanes = slice(i * CH, (i + 1) * CH)
                act_b[j, at : at + PART, lanes] = part.astype(BF)
                late = jnp.concatenate([carry[i], part[: PART - PAIRS]], axis=0)
                act_a[j, at : at + PART, lanes] = late.astype(BF)
                carry[i] = part[PART - PAIRS :]
        for i in range(4):
            act_a[j, HALF : HALF + 2 * PAIRS, i * CH : (i + 1) * CH] = jnp.concatenate(
                [carry[i], blank], axis=0
            ).astype(BF)

    def conv_frame(j, weight):
        taps = []
        for kt in range(LAGS):
            p = picked(j, 2 - kt, 2)
            taps += [act_a[p, 0:HALF], act_b[p], act_a[p, 2 * PAIRS : 2 * PAIRS + HALF]]
        both = jnp.dot(
            jnp.concatenate(taps, axis=1),
            weight[...].reshape(9 * 4 * CH, 2 * CH),
            preferred_element_type=F32,
        )
        return both[:, :CH], both[:, CH:]

    rows = [
        frame_stats(*[base[i, (j + 2) * HALF : (j + 3) * HALF, :] for i in range(2)])
        for j in range(span)
    ]
    stat_copies = share_stats(stats1, 0, rows)
    base_frames(0, 2)
    means, scales = norm_terms(stats1, 0, stat_copies)
    for j in range(span + 2):
        activate(
            j, lambda i, at: base[i, at : at + PART, :], j * HALF, means[j], scales[j], vecs[1], vecs[2]
        )
    weight_copies[0].wait()
    weight_copies[1].wait()

    halo = pltpu.make_async_remote_copy(
        src_ref=mid_send,
        dst_ref=mid_halo,
        send_sem=halo_send,
        recv_sem=halo_recv,
        device_id=(me, t + 1),
        device_id_type=MESH,
    )
    rows = [None] * span
    order = list(range(span - 2, span)) + list(range(span - 2))
    for at, j in enumerate(order):
        pieces = []
        for i, x in enumerate(conv_frame(j + 2, w1)):
            x = x.astype(BF)
            if at < 2:
                mid_send[at, i] = x
            x = x.astype(F32)
            mid[i, j * HALF : (j + 1) * HALF, :] = x
            pieces.append(x)
        rows[j] = frame_stats(*pieces)
        if at == 1:

            @pl.when(t < n_tm - 1)
            def _():
                halo.start()

    stat_copies2 = share_stats(stats2, 1, rows)
    means, scales = norm_terms(stats2, 1, stat_copies2)
    for j in range(span):
        activate(
            j + 2,
            lambda i, at: mid[i, at : at + PART, :],
            j * HALF,
            means[j + 2],
            scales[j + 2],
            vecs[3],
            vecs[4],
        )

    @pl.when(t > 0)
    def _():
        halo.wait_recv()

    for j in range(2):
        activate(
            j,
            lambda i, at: mid_halo[j, i, at : at + PART, :].astype(F32),
            0,
            means[j],
            scales[j],
            vecs[3],
            vecs[4],
        )
    weight_copies[2].wait()
    weight_copies[3].wait()
    for j in range(span):
        for i, x in enumerate(conv_frame(j + 2, w2)):
            x = x + base[i, (j + 2) * HALF : (j + 3) * HALF, :]
            resid[i, j * HALF : (j + 1) * HALF, :] = x.astype(BF).astype(F32)

    weight_copies[4].wait()
    cells = span * HALF
    spot = lax.broadcasted_iota(jnp.int32, (cells, CH), 0) & (PAIRS - 1)
    taps = [None] * 9
    even, odd = resid[0], resid[1]
    next_even = jnp.where(spot == PAIRS - 1, 0.0, pltpu.roll(even, cells - 1, axis=0))
    for kx, x in enumerate((even, odd, next_even)):
        x = x.reshape(span, HS // 2, 2, PAIRS, CH)
        upper, lower = x[:, :, 0], x[:, :, 1]
        below = jnp.concatenate([upper[:, 1:], jnp.zeros((span, 1, PAIRS, CH), F32)], axis=1)
        for ky, rows in enumerate((upper, lower, below)):
            taps[ky * 3 + kx] = rows.reshape(cells // 2, CH).astype(BF)
    encoded = jnp.dot(jnp.concatenate(taps, axis=1), wd[...], preferred_element_type=F32).astype(BF)
    unit_rows = RB * PW // 4
    latent[0:units] = encoded.reshape(units, unit_rows, CH)
    latent[units:] = jnp.zeros((cap, unit_rows, CH), BF)

    back = []
    for k in range(n_dp):
        d = lax.rem(me + k, n_dp)
        block = latent[pl.ds(recv_start_of(d, me), cap)]
        if k == 0:
            returned[me] = block
        else:
            packed[k] = block
            copy = pltpu.make_async_remote_copy(
                src_ref=packed.at[k],
                dst_ref=returned.at[me],
                send_sem=back_send.at[k],
                recv_sem=back_recv.at[me],
                device_id=(d, t),
                device_id_type=MESH,
            )
            copy.start()
            back.append(copy)
    for k in range(1, n_dp):
        d = lax.rem(me + k, n_dp)
        pltpu.make_async_copy(returned.at[d], returned.at[d], back_recv.at[d]).wait()
    for p in range(units):
        owner = jnp.int32(0)
        first = jnp.int32(0)
        for e in range(1, n_dp):
            later = send_start[e] <= p
            owner = jnp.where(later, e, owner)
            first = jnp.where(later, send_start[e], first)
        gathered[p * unit_rows : (p + 1) * unit_rows, :] = returned[
            owner, jnp.minimum(p - first, cap - 1)
        ].astype(F32)
    for k in range(unit_rows):
        out[:, k * CH : (k + 1) * CH] = gathered[pl.ds(k, units, stride=unit_rows), :].astype(BF)

    for copy in stat_copies + stat_copies2 + back:
        copy.wait_send()
    for k in range(n_dp):
        e = lax.rem(me + k, n_dp)
        if k:
            pixel_copy(e, 0).wait_send()

    @pl.when(t < n_tm - 1)
    def _():
        halo.wait_send()
        for k in range(n_dp):
            pixel_copy(lax.rem(me + k, n_dp), 1).wait_send()


def per_device(
    pixels,
    counts,
    clip_lengths,
    in_weight,
    in_bias,
    norm1_gain,
    norm1_bias,
    conv1_weight,
    norm2_gain,
    norm2_bias,
    conv2_weight,
    down_weight,
):
    n_dp = lax.axis_size("dp")
    n_tm = lax.axis_size("tm")
    units = pixels.shape[2]
    span = units // (HS // RB)
    cap = units // n_dp + 1
    unit_rows = RB * PW // 4
    vmem = pl.BlockSpec(memory_space=pltpu.VMEM)
    hbm = pl.BlockSpec(memory_space=pltpu.MemorySpace.HBM)
    result = pl.pallas_call(
        functools.partial(kernel, n_dp, n_tm),
        out_shape=jax.ShapeDtypeStruct((units, unit_rows * CH), BF),
        in_specs=[hbm] * 13,
        out_specs=vmem,
        scratch_shapes=[
            pltpu.SMEM((n_dp, n_dp), jnp.int32),
            pltpu.SMEM(clip_lengths.shape, jnp.int32),
            pltpu.VMEM(pixels.shape[2:], BF),
            pltpu.VMEM((LAGS * WIDE, CH), jnp.int32),
            pltpu.VMEM(in_weight.shape, BF),
            pltpu.VMEM((5, 1, CH), F32),
            pltpu.VMEM((CH, CH), F32),
            pltpu.VMEM((9, 4 * CH, 2 * CH), BF),
            pltpu.VMEM((9, 4 * CH, 2 * CH), BF),
            pltpu.VMEM((9 * CH, CH), BF),
            pltpu.VMEM((LAGS * WIDE, PW * CH), BF),
            pltpu.VMEM((n_dp, units, WIDE), BF),
            pltpu.VMEM((2, n_dp, units, WIDE), BF),
            pltpu.VMEM((2, 2 * units * RB, CH), F32),
            pltpu.VMEM((2 * span, HS, WIDE), BF),
            pltpu.VMEM(((span + 2) * HS, LAGS * WIDE), BF),
            pltpu.VMEM((2, (span + 2) * HALF, CH), F32),
            pltpu.VMEM((2, span * HALF, CH), F32),
            pltpu.VMEM((span + 2, HALF + 2 * PAIRS, 4 * CH), BF),
            pltpu.VMEM((span + 2, HALF, 4 * CH), BF),
            pltpu.VMEM((2, span * HALF, CH), F32),
            pltpu.VMEM((2, 2, HALF, CH), BF),
            pltpu.VMEM((2, 2, HALF, CH), BF),
            pltpu.VMEM((n_tm, 2 * span, CH), F32),
            pltpu.VMEM((n_tm, 2 * span, CH), F32),
            pltpu.VMEM((units + cap, unit_rows, CH), BF),
            pltpu.VMEM((n_dp, cap, unit_rows, CH), BF),
            pltpu.VMEM((n_dp, cap, unit_rows, CH), BF),
            pltpu.VMEM((units * unit_rows, CH), F32),
            pltpu.SemaphoreType.DMA((10,)),
            pltpu.SemaphoreType.DMA((5,)),
            pltpu.SemaphoreType.DMA((2, n_dp)),
            pltpu.SemaphoreType.DMA((2, n_dp)),
            pltpu.SemaphoreType.DMA((2, n_tm)),
            pltpu.SemaphoreType.DMA((2, n_tm)),
            pltpu.SemaphoreType.DMA(()),
            pltpu.SemaphoreType.DMA(()),
            pltpu.SemaphoreType.DMA((n_dp,)),
            pltpu.SemaphoreType.DMA((n_dp,)),
        ],
        compiler_params=pltpu.CompilerParams(
            collective_id=0, has_side_effects=True, vmem_limit_bytes=63 * 1024 * 1024
        ),
        name="encoder_block",
    )(
        counts,
        clip_lengths,
        pixels,
        jnp.asarray(tap_columns()),
        in_weight,
        *[v.reshape(1, CH) for v in (in_bias, norm1_gain, norm1_bias, norm2_gain, norm2_bias)],
        conv1_weight.reshape(9, 3 * CH, CH),
        conv2_weight.reshape(9, 3 * CH, CH),
        down_weight.reshape(9 * CH, CH),
    )
    return result.reshape(1, 1, units, unit_rows * CH)


def solution(mesh):
    in_specs = (
        P("dp", "tm", None, None),
        P("tm", None, None),
        P("dp", None),
        P(),
        P(),
        P(),
        P(),
        P(),
        P(),
        P(),
        P(),
        P(),
    )
    out_specs = P("dp", "tm", None, None)
    return jax.shard_map(
        per_device, mesh=mesh, in_specs=in_specs, out_specs=out_specs, check_vma=False
    )
```

```python
import functools

import jax
import jax.numpy as jnp
import numpy as np
from jax import lax
from jax.experimental import pallas as pl
from jax.experimental.pallas import tpu as pltpu
from jax.sharding import PartitionSpec as P

GROUPS = 32
HS = 32
PW = 16
RB = 4
CH = 128
LAGS = 3
EPS = 1e-06
MESH = pl.DeviceIdType.MESH
BF = jnp.bfloat16
F32 = jnp.float32
WIDE = 256
ROW = PW * 3
PIX = HS * PW
HALF = PIX // 2
PAIRS = PW // 2
PART = 64


def tap_columns():
    table = np.full((LAGS * WIDE, CH), -100, np.int32)
    for kt in range(LAGS):
        for dy in range(3):
            for col in range(PW):
                for color in range(3):
                    r = kt * WIDE + dy * ROW + col * 3 + color
                    for dx in range(3):
                        table[r, ((kt * 3 + dy) * 3 + dx) * 4 + color] = col + 1 - dx
    return table


def group_sum(x):
    lane = lax.broadcasted_iota(jnp.int32, x.shape, 1)
    for step in (1, 2):
        ahead = pltpu.roll(x, CH - step, axis=1)
        behind = pltpu.roll(x, step, axis=1)
        x = x + jnp.where((lane & step) == 0, ahead, behind)
    return x


def kernel(
    n_dp,
    n_tm,
    counts_hbm,
    lengths_hbm,
    pixels_hbm,
    columns_hbm,
    in_w_hbm,
    bias0_hbm,
    gain1_hbm,
    bias1_hbm,
    gain2_hbm,
    bias2_hbm,
    w1_hbm,
    w2_hbm,
    wd_hbm,
    out,
    counts,
    lengths,
    pixels,
    columns,
    in_w,
    vecs,
    taps_w,
    w1,
    w2,
    wd,
    toeplitz,
    placed,
    pix_in,
    pix_rows,
    xrows,
    lhs,
    base,
    mid,
    act_a,
    act_b,
    resid,
    mid_send,
    mid_halo,
    stats1,
    stats2,
    latent,
    packed,
    returned,
    gathered,
    small_sem,
    w_sem,
    px_send,
    px_recv,
    st_send,
    st_recv,
    halo_send,
    halo_recv,
    back_send,
    back_recv,
):
    units = pixels.shape[0]
    per_frame = HS // RB
    span = units // per_frame
    cap = units // n_dp + 1
    me = lax.axis_index("dp")
    t = lax.axis_index("tm")
    clips = lengths.shape[1]

    barrier = pltpu.get_barrier_semaphore()

    def greet(d, column):
        pl.semaphore_signal(barrier, inc=1, device_id=(d, column), device_id_type=MESH)

    for k in range(1, n_tm):
        greet(me, lax.rem(t + k, n_tm))
    for k in range(1, n_dp):
        d = lax.rem(me + k, n_dp)
        greet(d, t)

        @pl.when(t > 0)
        def _():
            greet(d, t - 1)

        @pl.when(t < n_tm - 1)
        def _():
            greet(d, t + 1)

    small = (
        (pixels_hbm.at[0, 0], pixels),
        (counts_hbm.at[0], counts),
        (columns_hbm, columns),
        (in_w_hbm, in_w),
        (lengths_hbm, lengths),
        (bias0_hbm, vecs.at[0]),
        (gain1_hbm, vecs.at[1]),
        (bias1_hbm, vecs.at[2]),
        (gain2_hbm, vecs.at[3]),
        (bias2_hbm, vecs.at[4]),
    )
    small_copies = [
        pltpu.make_async_copy(src, dst, small_sem.at[i]) for i, (src, dst) in enumerate(small)
    ]
    for copy in small_copies:
        copy.start()
    side = 3 * CH
    large = (
        (w1_hbm, w1.at[:, 0:side, 0:CH]),
        (w1_hbm, w1.at[:, CH : CH + side, CH : 2 * CH]),
        (w2_hbm, w2.at[:, 0:side, 0:CH]),
        (w2_hbm, w2.at[:, CH : CH + side, CH : 2 * CH]),
        (wd_hbm, wd),
    )
    weight_copies = [
        pltpu.make_async_copy(src, dst, w_sem.at[i]) for i, (src, dst) in enumerate(large)
    ]
    for copy in weight_copies:
        copy.start()
    small_copies[0].wait()
    small_copies[1].wait()

    def recv_start_of(d, e):
        total = jnp.int32(0)
        for other in range(n_dp):
            total = total + jnp.where(other < d, counts[other, e], 0)
        return total

    send_start, send_end = [], []
    running = jnp.int32(0)
    for e in range(n_dp):
        send_start.append(running)
        running = running + counts[me, e]
        send_end.append(running)

    place_r = lax.broadcasted_iota(jnp.int32, (units, units), 0)
    place_i = lax.broadcasted_iota(jnp.int32, (units, units), 1)
    mine = pixels[...]
    for e in range(n_dp):
        turn = recv_start_of(me, e) - send_start[e]
        hit = (place_r == place_i + turn) & (place_i >= send_start[e]) & (place_i < send_end[e])
        placed[e, :, 0 : RB * ROW] = jnp.dot(
            hit.astype(F32).astype(BF), mine, preferred_element_type=F32
        ).astype(BF)

    at_edge = (t == 0) | (t == n_tm - 1)

    @pl.when(at_edge)
    def _():
        pl.semaphore_wait(barrier, n_tm - 1 + 2 * (n_dp - 1))

    @pl.when(jnp.logical_not(at_edge))
    def _():
        pl.semaphore_wait(barrier, n_tm - 1 + 3 * (n_dp - 1))

    def pixel_copy(e, ahead):
        return pltpu.make_async_remote_copy(
            src_ref=placed.at[e],
            dst_ref=pix_in.at[1 - ahead, me],
            send_sem=px_send.at[ahead, e],
            recv_sem=px_recv.at[1 - ahead, me],
            device_id=(e, t + ahead),
            device_id_type=MESH,
        )

    for k in range(n_dp):
        e = lax.rem(me + k, n_dp)

        @pl.when(t < n_tm - 1)
        def _():
            pixel_copy(e, 1).start()

        if k:
            pixel_copy(e, 0).start()
    pix_in[1, me] = placed[me]

    @pl.when(t == 0)
    def _():
        pix_in[0] = jnp.zeros(pix_in.shape[1:], BF)
        mid_halo[...] = jnp.zeros(mid_halo.shape, BF)

    for copy in small_copies[2:]:
        copy.wait()
    taps_w[...] = jnp.zeros(taps_w.shape, F32)
    for tap in range(27):
        kt, dy, dx = tap // 9, tap // 3 % 3, tap % 3
        taps_w[4 * tap : 4 * tap + 3, :] = in_w[kt, dy, dx].astype(F32)
    place = columns[...]
    weight_in = taps_w[...].astype(BF)
    for col in range(PW):
        pick = jnp.where(place == col, 1.0, 0.0).astype(BF)
        toeplitz[:, col * CH : (col + 1) * CH] = jnp.dot(
            pick, weight_in, preferred_element_type=F32
        ).astype(BF)
    for weight in (w1, w2):
        weight[:, side : side + CH, 0:CH] = jnp.zeros((9, CH, CH), BF)
        weight[:, 0:CH, CH : 2 * CH] = jnp.zeros((9, CH, CH), BF)

    start = t * span
    ends, begins = [], []
    running = jnp.int32(0)
    for k in range(clips):
        begins.append(running)
        running = running + lengths[0, k]
        ends.append(running)

    def clip_of(g):
        first, last = begins[0], ends[0]
        for k in range(1, clips):
            later = ends[k - 1] <= g
            first = jnp.where(later, begins[k], first)
            last = jnp.where(later, ends[k], last)
        return first, last

    frame_clip = [clip_of(start - 2 + j) for j in range(span + 2)]

    def picked(j, lag, lead):
        g = start - 2 + j
        return jnp.maximum(g - lag, frame_clip[j][0]) - (start - lead)

    for k in range(1, n_dp):
        d = lax.rem(me + k, n_dp)
        pltpu.make_async_copy(pix_in.at[1, d], pix_in.at[1, d], px_recv.at[1, d]).wait()

    @pl.when(t > 0)
    def _():
        for d in range(n_dp):
            pltpu.make_async_copy(pix_in.at[0, d], pix_in.at[0, d], px_recv.at[0, d]).wait()

    whole = []
    for half in range(2):
        total = pix_in[half, 0].astype(F32)
        for d in range(1, n_dp):
            total = total + pix_in[half, d].astype(F32)
        whole.append(total)
    whole = jnp.concatenate(whole, axis=0)
    lane = lax.broadcasted_iota(jnp.int32, whole.shape, 1)
    for q in range(RB):
        shifted = pltpu.roll(whole, (ROW - q * ROW) % WIDE, axis=1)
        rows = jnp.where((lane >= ROW) & (lane < 2 * ROW), shifted, 0.0)
        for half in range(2):
            pix_rows[half, pl.ds(q, 2 * units, stride=RB), :] = rows[:, half * CH : (half + 1) * CH]
    rows = jnp.concatenate([pix_rows[0], pix_rows[1]], axis=1)
    place = lax.broadcasted_iota(jnp.int32, rows.shape, 0) & (HS - 1)
    count = rows.shape[0]
    above = jnp.where(place == 0, 0.0, pltpu.roll(rows, 1, axis=0))
    below = jnp.where(place == HS - 1, 0.0, pltpu.roll(rows, count - 1, axis=0))
    rows = rows + pltpu.roll(above, WIDE - ROW, axis=1) + pltpu.roll(below, ROW, axis=1)
    xrows[...] = rows.astype(BF).reshape(2 * span, HS, WIDE)

    for j in range(span + 2):
        for kt in range(LAGS):
            lhs[j * HS : (j + 1) * HS, kt * WIDE : (kt + 1) * WIDE] = xrows[picked(j, 2 - kt, 4)]

    def base_frames(first, amount):
        patch = lhs[first * HS : (first + amount) * HS, :]
        for pair in range(PAIRS):
            both = jnp.dot(
                patch, toeplitz[:, pair * 2 * CH : (pair + 1) * 2 * CH], preferred_element_type=F32
            )
            for side_at in range(2):
                part = both[:, side_at * CH : (side_at + 1) * CH] + vecs[0]
                base[side_at, pl.ds(first * HALF + pair, amount * HS, stride=PAIRS), :] = part.astype(
                    BF
                ).astype(F32)

    base_frames(2, span)

    def frame_stats(even, odd):
        total = jnp.sum(even, axis=0, keepdims=True) + jnp.sum(odd, axis=0, keepdims=True)
        mean = total * (1.0 / PIX)
        even, odd = even - mean, odd - mean
        away = jnp.sum(even * even, axis=0, keepdims=True) + jnp.sum(odd * odd, axis=0, keepdims=True)
        return total, away

    def share_stats(stats, which, rows):
        stats[t] = jnp.concatenate([r[0] for r in rows] + [r[1] for r in rows], axis=0)
        copies = []
        for k in range(1, n_tm):
            other = lax.rem(t + k, n_tm)
            copy = pltpu.make_async_remote_copy(
                src_ref=stats.at[t],
                dst_ref=stats.at[t],
                send_sem=st_send.at[which, k],
                recv_sem=st_recv.at[which, t],
                device_id=(me, other),
                device_id_type=MESH,
            )
            copy.start()
            copies.append(copy)
        return copies

    def norm_terms(stats, which, copies):
        for k in range(1, n_tm):
            other = lax.rem(t + k, n_tm)
            pltpu.make_async_copy(stats.at[other], stats.at[other], st_recv.at[which, other]).wait()
        sums = jnp.concatenate([stats[i, 0:span] for i in range(n_tm)], axis=0)
        devs = jnp.concatenate([stats[i, span : 2 * span] for i in range(n_tm)], axis=0)
        g = lax.broadcasted_iota(jnp.int32, sums.shape, 0)
        share = CH // GROUPS
        inside, sizes, means = [], [], []
        for first, last in frame_clip:
            hit = (g >= first) & (g < last)
            inside.append(hit)
            sizes.append((last - first).astype(F32) * (PIX * share))
            means.append(jnp.sum(jnp.where(hit, sums, 0.0), axis=0, keepdims=True))
        pad = [jnp.zeros((8 - len(means), CH), F32)] if len(means) < 8 else []
        means = group_sum(jnp.concatenate(means + pad, axis=0))
        means = [means[j : j + 1] / sizes[j] for j in range(span + 2)]
        frame_mean = sums * (1.0 / PIX)
        spread = []
        for j in range(span + 2):
            off = frame_mean - means[j]
            spread.append(
                jnp.sum(jnp.where(inside[j], devs + PIX * off * off, 0.0), axis=0, keepdims=True)
            )
        spread = group_sum(jnp.concatenate(spread + pad, axis=0))
        scales = [lax.rsqrt(spread[j : j + 1] / sizes[j] + EPS) for j in range(span + 2)]
        return means, scales

    pair_at = lax.broadcasted_iota(jnp.int32, (PART, CH), 0) & (PAIRS - 1)
    blank = jnp.zeros((PAIRS, CH), F32)

    def activate(j, source, first, mean, scale, gain, bias):
        factor = scale * (0.5 * gain)
        shift = 0.5 * bias
        carry = [blank] * 4
        for at in range(0, HALF, PART):
            done = []
            for side_at in range(2):
                x = source(side_at, first + at)
                y = (x - mean) * factor + shift
                done.append(y + y * jnp.tanh(y))
            even, odd = done
            before = jnp.where(pair_at == 0, 0.0, pltpu.roll(odd, 1, axis=0))
            after = jnp.where(pair_at == PAIRS - 1, 0.0, pltpu.roll(even, PART - 1, axis=0))
            for i, part in enumerate((before, even, odd, after)):
                lanes = slice(i * CH, (i + 1) * CH)
                act_b[j, at : at + PART, lanes] = part.astype(BF)
                late = jnp.concatenate([carry[i], part[: PART - PAIRS]], axis=0)
                act_a[j, at : at + PART, lanes] = late.astype(BF)
                carry[i] = part[PART - PAIRS :]
        for i in range(4):
            act_a[j, HALF : HALF + 2 * PAIRS, i * CH : (i + 1) * CH] = jnp.concatenate(
                [carry[i], blank], axis=0
            ).astype(BF)

    def conv_frames(frames, weight):
        taps = []
        for kt in range(LAGS):
            picks = [picked(j, 2 - kt, 2) for j in frames]
            taps += [
                jnp.concatenate([act_a[p, 0:HALF] for p in picks], axis=0),
                jnp.concatenate([act_b[p] for p in picks], axis=0),
                jnp.concatenate([act_a[p, 2 * PAIRS : 2 * PAIRS + HALF] for p in picks], axis=0),
            ]
        both = jnp.dot(
            jnp.concatenate(taps, axis=1),
            weight[...].reshape(9 * 4 * CH, 2 * CH),
            preferred_element_type=F32,
        )
        return [
            [both[i * HALF : (i + 1) * HALF, :CH], both[i * HALF : (i + 1) * HALF, CH:]]
            for i in range(len(frames))
        ]

    rows = [
        frame_stats(*[base[i, (j + 2) * HALF : (j + 3) * HALF, :] for i in range(2)])
        for j in range(span)
    ]
    stat_copies = share_stats(stats1, 0, rows)
    base_frames(0, 2)
    means, scales = norm_terms(stats1, 0, stat_copies)
    for j in range(span + 2):
        activate(
            j, lambda i, at: base[i, at : at + PART, :], j * HALF, means[j], scales[j], vecs[1], vecs[2]
        )
    weight_copies[0].wait()
    weight_copies[1].wait()

    halo = pltpu.make_async_remote_copy(
        src_ref=mid_send,
        dst_ref=mid_halo,
        send_sem=halo_send,
        recv_sem=halo_recv,
        device_id=(me, t + 1),
        device_id_type=MESH,
    )
    rows = [None] * span
    order = list(range(span - 2, span)) + list(range(span - 2))
    for at in range(0, span, 2):
        pair = order[at : at + 2]
        for which, (j, sides) in enumerate(zip(pair, conv_frames([j + 2 for j in pair], w1))):
            pieces = []
            for i, x in enumerate(sides):
                x = x.astype(BF)
                if at == 0:
                    mid_send[which, i] = x
                x = x.astype(F32)
                mid[i, j * HALF : (j + 1) * HALF, :] = x
                pieces.append(x)
            rows[j] = frame_stats(*pieces)
        if at == 0:

            @pl.when(t < n_tm - 1)
            def _():
                halo.start()

    stat_copies2 = share_stats(stats2, 1, rows)
    means, scales = norm_terms(stats2, 1, stat_copies2)
    for j in range(span):
        activate(
            j + 2,
            lambda i, at: mid[i, at : at + PART, :],
            j * HALF,
            means[j + 2],
            scales[j + 2],
            vecs[3],
            vecs[4],
        )

    @pl.when(t > 0)
    def _():
        halo.wait_recv()

    for j in range(2):
        activate(
            j,
            lambda i, at: mid_halo[j, i, at : at + PART, :].astype(F32),
            0,
            means[j],
            scales[j],
            vecs[3],
            vecs[4],
        )
    weight_copies[2].wait()
    weight_copies[3].wait()
    for at in range(0, span, 2):
        pair = [at, at + 1]
        for j, sides in zip(pair, conv_frames([j + 2 for j in pair], w2)):
            for i, x in enumerate(sides):
                x = x + base[i, (j + 2) * HALF : (j + 3) * HALF, :]
                resid[i, j * HALF : (j + 1) * HALF, :] = x.astype(BF).astype(F32)

    weight_copies[4].wait()
    cells = span * HALF
    spot = lax.broadcasted_iota(jnp.int32, (cells, CH), 0) & (PAIRS - 1)
    taps = [None] * 9
    even, odd = resid[0], resid[1]
    next_even = jnp.where(spot == PAIRS - 1, 0.0, pltpu.roll(even, cells - 1, axis=0))
    for kx, x in enumerate((even, odd, next_even)):
        x = x.reshape(span, HS // 2, 2, PAIRS, CH)
        upper, lower = x[:, :, 0], x[:, :, 1]
        below = jnp.concatenate([upper[:, 1:], jnp.zeros((span, 1, PAIRS, CH), F32)], axis=1)
        for ky, rows in enumerate((upper, lower, below)):
            taps[ky * 3 + kx] = rows.reshape(cells // 2, CH).astype(BF)
    encoded = jnp.dot(jnp.concatenate(taps, axis=1), wd[...], preferred_element_type=F32).astype(BF)
    unit_rows = RB * PW // 4
    latent[0:units] = encoded.reshape(units, unit_rows, CH)
    latent[units:] = jnp.zeros((cap, unit_rows, CH), BF)

    back = []
    for k in range(n_dp):
        d = lax.rem(me + k, n_dp)
        block = latent[pl.ds(recv_start_of(d, me), cap)]
        if k == 0:
            returned[me] = block
        else:
            packed[k] = block
            copy = pltpu.make_async_remote_copy(
                src_ref=packed.at[k],
                dst_ref=returned.at[me],
                send_sem=back_send.at[k],
                recv_sem=back_recv.at[me],
                device_id=(d, t),
                device_id_type=MESH,
            )
            copy.start()
            back.append(copy)
    for k in range(1, n_dp):
        d = lax.rem(me + k, n_dp)
        pltpu.make_async_copy(returned.at[d], returned.at[d], back_recv.at[d]).wait()
    for p in range(units):
        owner = jnp.int32(0)
        first = jnp.int32(0)
        for e in range(1, n_dp):
            later = send_start[e] <= p
            owner = jnp.where(later, e, owner)
            first = jnp.where(later, send_start[e], first)
        gathered[p * unit_rows : (p + 1) * unit_rows, :] = returned[
            owner, jnp.minimum(p - first, cap - 1)
        ].astype(F32)
    for k in range(unit_rows):
        out[:, k * CH : (k + 1) * CH] = gathered[pl.ds(k, units, stride=unit_rows), :].astype(BF)

    for copy in stat_copies + stat_copies2 + back:
        copy.wait_send()
    for k in range(n_dp):
        e = lax.rem(me + k, n_dp)
        if k:
            pixel_copy(e, 0).wait_send()

    @pl.when(t < n_tm - 1)
    def _():
        halo.wait_send()
        for k in range(n_dp):
            pixel_copy(lax.rem(me + k, n_dp), 1).wait_send()


def per_device(
    pixels,
    counts,
    clip_lengths,
    in_weight,
    in_bias,
    norm1_gain,
    norm1_bias,
    conv1_weight,
    norm2_gain,
    norm2_bias,
    conv2_weight,
    down_weight,
):
    n_dp = lax.axis_size("dp")
    n_tm = lax.axis_size("tm")
    units = pixels.shape[2]
    span = units // (HS // RB)
    cap = units // n_dp + 1
    unit_rows = RB * PW // 4
    vmem = pl.BlockSpec(memory_space=pltpu.VMEM)
    hbm = pl.BlockSpec(memory_space=pltpu.MemorySpace.HBM)
    result = pl.pallas_call(
        functools.partial(kernel, n_dp, n_tm),
        out_shape=jax.ShapeDtypeStruct((units, unit_rows * CH), BF),
        in_specs=[hbm] * 13,
        out_specs=vmem,
        scratch_shapes=[
            pltpu.SMEM((n_dp, n_dp), jnp.int32),
            pltpu.SMEM(clip_lengths.shape, jnp.int32),
            pltpu.VMEM(pixels.shape[2:], BF),
            pltpu.VMEM((LAGS * WIDE, CH), jnp.int32),
            pltpu.VMEM(in_weight.shape, BF),
            pltpu.VMEM((5, 1, CH), F32),
            pltpu.VMEM((CH, CH), F32),
            pltpu.VMEM((9, 4 * CH, 2 * CH), BF),
            pltpu.VMEM((9, 4 * CH, 2 * CH), BF),
            pltpu.VMEM((9 * CH, CH), BF),
            pltpu.VMEM((LAGS * WIDE, PW * CH), BF),
            pltpu.VMEM((n_dp, units, WIDE), BF),
            pltpu.VMEM((2, n_dp, units, WIDE), BF),
            pltpu.VMEM((2, 2 * units * RB, CH), F32),
            pltpu.VMEM((2 * span, HS, WIDE), BF),
            pltpu.VMEM(((span + 2) * HS, LAGS * WIDE), BF),
            pltpu.VMEM((2, (span + 2) * HALF, CH), F32),
            pltpu.VMEM((2, span * HALF, CH), F32),
            pltpu.VMEM((span + 2, HALF + 2 * PAIRS, 4 * CH), BF),
            pltpu.VMEM((span + 2, HALF, 4 * CH), BF),
            pltpu.VMEM((2, span * HALF, CH), F32),
            pltpu.VMEM((2, 2, HALF, CH), BF),
            pltpu.VMEM((2, 2, HALF, CH), BF),
            pltpu.VMEM((n_tm, 2 * span, CH), F32),
            pltpu.VMEM((n_tm, 2 * span, CH), F32),
            pltpu.VMEM((units + cap, unit_rows, CH), BF),
            pltpu.VMEM((n_dp, cap, unit_rows, CH), BF),
            pltpu.VMEM((n_dp, cap, unit_rows, CH), BF),
            pltpu.VMEM((units * unit_rows, CH), F32),
            pltpu.SemaphoreType.DMA((10,)),
            pltpu.SemaphoreType.DMA((5,)),
            pltpu.SemaphoreType.DMA((2, n_dp)),
            pltpu.SemaphoreType.DMA((2, n_dp)),
            pltpu.SemaphoreType.DMA((2, n_tm)),
            pltpu.SemaphoreType.DMA((2, n_tm)),
            pltpu.SemaphoreType.DMA(()),
            pltpu.SemaphoreType.DMA(()),
            pltpu.SemaphoreType.DMA((n_dp,)),
            pltpu.SemaphoreType.DMA((n_dp,)),
        ],
        compiler_params=pltpu.CompilerParams(
            collective_id=0, has_side_effects=True, vmem_limit_bytes=63 * 1024 * 1024
        ),
        name="encoder_block",
    )(
        counts,
        clip_lengths,
        pixels,
        jnp.asarray(tap_columns()),
        in_weight,
        *[v.reshape(1, CH) for v in (in_bias, norm1_gain, norm1_bias, norm2_gain, norm2_bias)],
        conv1_weight.reshape(9, 3 * CH, CH),
        conv2_weight.reshape(9, 3 * CH, CH),
        down_weight.reshape(9 * CH, CH),
    )
    return result.reshape(1, 1, units, unit_rows * CH)


def solution(mesh):
    in_specs = (
        P("dp", "tm", None, None),
        P("tm", None, None),
        P("dp", None),
        P(),
        P(),
        P(),
        P(),
        P(),
        P(),
        P(),
        P(),
        P(),
    )
    out_specs = P("dp", "tm", None, None)
    return jax.shard_map(
        per_device, mesh=mesh, in_specs=in_specs, out_specs=out_specs, check_vma=False
    )
```
